32 devices in a mesh: lat: 4 (over y, x), lon: 8 (over z, core).
Axes of the slice: x: 2, y: 2, z: 4, core: 2. Of those that a mesh axis runs over, the one named last changes fastest.
Arguments:
- features: bfloat16 [4, 24, 96, 192], P(None, 'lat', 'lon'), may hold values from -6 to 6
- norm_gain: float32 [192], replicated, may hold values from 0.5 to 1.5
- norm_shift: float32 [192], replicated, may hold values from -3 to 3
- w_qkv: bfloat16 [192, 576], replicated, may hold values from -0.4375 to 0.4375
- w_out: bfloat16 [192, 192], replicated, may hold values from -0.4375 to 0.4375
- bias_table: float32 [2, 4, 6, 3312], P(None, 'lat'), may hold values from -3 to 400
- index_table: int32 [144, 144], replicated, may hold values from 0 to 3311, as said below
- cotangent: bfloat16 [4, 24, 96, 192], P(None, 'lat', 'lon'), may hold values from -6 to 6
Outputs:
- outputs: bfloat16 [4, 24, 96, 192], P(None, 'lat', 'lon')
- grad_features: bfloat16 [4, 24, 96, 192], P(None, 'lat', 'lon')
- grad_gain: float32 [192], replicated
- grad_shift: float32 [192], replicated
- grad_wqkv: float32 [192, 576], replicated
- grad_wout: float32 [192, 192], replicated
- grad_table: float32 [2, 4, 6, 3312], P(None, 'lat')
The draws below stay inside these ranges and needn't reach their ends.
Inputs may be any that keep to these rules, and one draw needn't show every extreme that they name: `index_table`: entry (i, j) labels the bias of tokens i and j of a window; two pairs share a label exactly when they have the same two levels, the same two rows and the same column difference.
All inputs are finite; a program needn't handle non-finite values.
Results may differ from the reference program's by a relative error of at most 0.018.
Values may be sent and summed in bfloat16 or wider, within the bound.
No kernel may reach another device: no remote copies, remote signals or barrier semaphores. Data moves between devices by JAX's collectives and lax.ppermute only.
A program may use at most 128 MiB of HBM per device.

```python
import jax
import jax.numpy as jnp
from jax import lax

D = 192
HEADS = 6
WZ = 2
WH = 6
WW = 12
WIN = 144
POS = 3312
LEVELS = 4
NLAT = 24
NLON = 96
LEVEL_WIN = 2
LAT_WIN = 4
TOKENS = 9216


def label_order(key):
    return jax.random.permutation(jax.random.fold_in(key, 17), POS)


def canonical_index():
    win_len = WZ * WH * WW
    tokens_at = jnp.arange(win_len, dtype=jnp.int32)
    level_pos = tokens_at // (WH * WW)
    lat_pos = tokens_at // WW % WH
    lon_pos = tokens_at % WW
    pair_block = (level_pos[:, None] * WZ + level_pos[None, :]) * (WH * WH) + lat_pos[:, None] * WH + lat_pos[None, :]
    return pair_block * (2 * WW - 1) + lon_pos[:, None] - lon_pos[None, :] + WW - 1


def draw_index_table(key, part):
    return label_order(key)[canonical_index()].astype(jnp.int32)


def draw_bias_table(key, part):
    full_shape = (LEVEL_WIN, LAT_WIN, HEADS, POS)
    return jnp.clip(jax.random.normal(jax.random.fold_in(key, 6), full_shape, jnp.float32), -3.0, 3.0)


def steps_of(key, extent, split, least, top_value):
    loudness, own = 1.0, jax.random.fold_in(key, 6)
    for axis_at, blocks in split:
        draws = jnp.exp(jax.random.uniform(jax.random.fold_in(own, axis_at), (blocks,), jnp.float32, least / len(split), top_value / len(split)))
        loudness = loudness * jnp.repeat(draws, extent[axis_at] // blocks).reshape([-1 if axis == axis_at else 1 for axis in range(len(extent))])
    return loudness


def scatter_about(stream_key, dims, deviation, limit, split=(), kind=jnp.bfloat16):
    drawn = deviation * jax.random.normal(stream_key, dims, jnp.float32)
    if split:
        drawn = drawn * steps_of(stream_key, dims, split, -0.22, 0.18)
    return jnp.clip(drawn, -limit, limit).astype(kind)


def setup_inputs(seed: int = 0) -> dict:
    splits = jax.random.split(jax.random.key(seed), 9)
    features = scatter_about(splits[0], (LEVELS, NLAT, NLON, D), 1.0, 6.0, ((1, 4), (2, 8)))
    norm_gain = jnp.clip(1.0 + 0.1 * jax.random.normal(splits[1], (D,), jnp.float32), 0.5, 1.5)
    norm_shift = scatter_about(splits[2], (D,), 0.5, 3.0, (), jnp.float32)
    w_qkv = scatter_about(splits[3], (D, 3 * D), D ** -0.5, 0.4375)
    w_out = scatter_about(splits[4], (D, D), D ** -0.5, 0.4375)
    bias_table = draw_bias_table(jax.random.fold_in(splits[8], 71), 0)
    index_table = draw_index_table(jax.random.fold_in(splits[8], 71), 0)
    cotangent = scatter_about(splits[7], (LEVELS, NLAT, NLON, D), 1.0, 6.0, ((1, 4), (2, 8)))
    return dict(features=features, norm_gain=norm_gain, norm_shift=norm_shift, w_qkv=w_qkv, w_out=w_out, bias_table=bias_table, index_table=index_table, cotangent=cotangent)


epsilon = 1e-05

def upcast(tensor):
    return lax.optimization_barrier(tensor).astype(jnp.float32)

def normalize(features, norm_gain, norm_shift):
    values = features.astype(jnp.float32)
    center = values - lax.optimization_barrier(jnp.mean(values, -1, keepdims=True))
    inv_std = lax.rsqrt(lax.optimization_barrier(jnp.mean(center * center, -1, keepdims=True)) + epsilon)
    x_hat = center * inv_std
    normed = (x_hat * norm_gain + norm_shift).astype(jnp.bfloat16)
    return (x_hat, inv_std, normed)

def norm_backward(grad_normed, x_hat, inv_std, norm_gain, cotangent):
    upstream = grad_normed.astype(jnp.float32)
    gain_part = lax.optimization_barrier(jnp.sum(upstream * x_hat, (0, 1, 2)))
    shift_part = lax.optimization_barrier(jnp.sum(upstream, (0, 1, 2)))
    g_hat = upstream * norm_gain
    centred = g_hat - lax.optimization_barrier(jnp.mean(g_hat, -1, keepdims=True)) - x_hat * lax.optimization_barrier(jnp.mean(g_hat * x_hat, -1, keepdims=True))
    grad_features = (cotangent.astype(jnp.float32) + inv_std * centred).astype(jnp.bfloat16)
    return (grad_features, gain_part, shift_part)

def to_windows(volume, level_win, lat_win, lon_win):
    channels = volume.shape[-1]
    volume = volume.reshape(level_win, WZ, lat_win, WH, lon_win, WW, channels)
    volume = volume.transpose(0, 2, 4, 1, 3, 5, 6)
    return volume.reshape(level_win, lat_win, lon_win, WZ * WH * WW, channels)

def from_windows(blocks):
    level_win, lat_win, lon_win = (blocks.shape[0], blocks.shape[1], blocks.shape[2])
    channels = blocks.shape[-1]
    blocks = blocks.reshape(level_win, lat_win, lon_win, WZ, WH, WW, channels)
    blocks = blocks.transpose(0, 3, 1, 4, 2, 5, 6)
    return blocks.reshape(level_win * WZ, lat_win * WH, lon_win * WW, channels)

def window_mask(lat_key, level_key, level_win, lat_win):
    grid_shape = (level_win, lat_win, WZ, WH, WW)
    per_level = jnp.broadcast_to(level_key.reshape(level_win, 1, WZ, 1, 1), grid_shape).reshape(level_win, lat_win, WZ * WH * WW)
    per_lat = jnp.broadcast_to(lat_key.reshape(1, lat_win, 1, WH, 1), grid_shape).reshape(level_win, lat_win, WZ * WH * WW)
    same_level = per_level[..., :, None] == per_level[..., None, :]
    same_lat = per_lat[..., :, None] == per_lat[..., None, :]
    return jnp.logical_and(same_level, same_lat)

def table_grad(score_grad, index_table):
    groups = score_grad.shape[0]
    pair_count = index_table.shape[0] * index_table.shape[1]
    columns = score_grad.reshape(groups * HEADS, pair_count).T
    summed = jax.ops.segment_sum(columns, index_table.reshape(pair_count), num_segments=POS)
    return summed.T.reshape(groups, HEADS, POS)

def attend(inputs_win, grad_win, pos_bias, allowed, w_qkv, w_out):
    win_count, win_len, channels = inputs_win.shape
    head_size = channels // HEADS
    scaling = head_size ** (-0.5)
    flat_in = inputs_win.reshape(win_count * win_len, channels)
    projected = jnp.dot(flat_in, w_qkv, preferred_element_type=jnp.float32).astype(jnp.bfloat16)
    projected = projected.reshape(win_count, win_len, 3, HEADS, head_size)
    query_part, key_part, value_part = (projected[:, :, 0], projected[:, :, 1], projected[:, :, 2])
    logits = jnp.einsum('bihe,bjhe->bhij', upcast(query_part), upcast(key_part)) * scaling + pos_bias
    logits = jnp.where(allowed[:, None], logits, -jnp.inf)
    row_max = lax.optimization_barrier(jnp.max(logits, -1, keepdims=True))
    raised = jnp.exp(logits - row_max)
    weights_f32 = raised / lax.optimization_barrier(jnp.sum(raised, -1, keepdims=True))
    weights_bf = weights_f32.astype(jnp.bfloat16)
    mixed_heads = jnp.einsum('bhij,bjhe->bihe', upcast(weights_bf), upcast(value_part)).astype(jnp.bfloat16)
    mixed_flat = mixed_heads.reshape(win_count * win_len, channels)
    attn_out = jnp.dot(mixed_flat, w_out, preferred_element_type=jnp.float32).astype(jnp.bfloat16)
    grad_flat = grad_win.reshape(win_count * win_len, channels)
    grad_wout = jnp.dot(mixed_flat.T, grad_flat, preferred_element_type=jnp.float32)
    grad_heads = jnp.dot(grad_flat, w_out.T, preferred_element_type=jnp.float32).astype(jnp.bfloat16)
    grad_heads = grad_heads.reshape(win_count, win_len, HEADS, head_size)
    grad_weights = jnp.einsum('bihe,bjhe->bhij', upcast(grad_heads), upcast(value_part))
    grad_value = jnp.einsum('bhij,bihe->bjhe', upcast(weights_bf), upcast(grad_heads)).astype(jnp.bfloat16)
    grad_logits = weights_f32 * (grad_weights - lax.optimization_barrier(jnp.sum(weights_f32 * grad_weights, -1, keepdims=True)))
    logit_bf = grad_logits.astype(jnp.bfloat16)
    grad_query = (jnp.einsum('bhij,bjhe->bihe', upcast(logit_bf), upcast(key_part)) * scaling).astype(jnp.bfloat16)
    grad_key = (jnp.einsum('bhij,bihe->bjhe', upcast(logit_bf), upcast(query_part)) * scaling).astype(jnp.bfloat16)
    grad_proj = jnp.stack((grad_query, grad_key, grad_value), 2).reshape(win_count * win_len, 3 * channels)
    grad_wqkv = jnp.dot(flat_in.T, grad_proj, preferred_element_type=jnp.float32)
    grad_input = jnp.dot(grad_proj, w_qkv.T, preferred_element_type=jnp.float32).astype(jnp.bfloat16)
    return (attn_out.reshape(win_count, win_len, channels), grad_input.reshape(win_count, win_len, channels), grad_wqkv, grad_wout, grad_logits)

def reference(features, norm_gain, norm_shift, w_qkv, w_out, bias_table, index_table, cotangent):
    levels, lat_rows, lon_cols, channels = features.shape
    level_win, lat_win, lon_win = (levels // WZ, lat_rows // WH, lon_cols // WW)
    offsets = (-(WZ // 2), -(WH // 2), -(WW // 2))
    returns = (WZ // 2, WH // 2, WW // 2)
    x_hat, inv_std, normed = normalize(features, norm_gain, norm_shift)
    shifted = jnp.roll(normed, offsets, (0, 1, 2))
    grad_shifted = jnp.roll(cotangent, offsets, (0, 1, 2))
    input_blocks = to_windows(shifted, level_win, lat_win, lon_win).transpose(1, 0, 2, 3, 4)
    input_blocks = input_blocks.reshape(lat_win, level_win * lon_win, WIN, channels)
    grad_blocks = to_windows(grad_shifted, level_win, lat_win, lon_win).transpose(1, 0, 2, 3, 4)
    grad_blocks = grad_blocks.reshape(lat_win, level_win * lon_win, WIN, channels)
    lat_index = jnp.arange(lat_rows, dtype=jnp.int32)
    lat_key = (lat_index >= lat_rows - WH // 2).astype(jnp.int32)
    level_key = (jnp.arange(levels, dtype=jnp.int32) >= levels - WZ // 2).astype(jnp.int32)
    allowed = window_mask(lat_key, level_key, level_win, lat_win).transpose(1, 0, 2, 3)
    table_rows = bias_table.transpose(1, 0, 2, 3)

    def one_row(inputs):
        input_row, grad_row, table_row, mask_row = inputs
        pos_bias = jnp.take(table_row, index_table, axis=2)
        pos_bias = jnp.broadcast_to(pos_bias[:, None], (level_win, lon_win, HEADS, WIN, WIN))
        pos_bias = pos_bias.reshape(level_win * lon_win, HEADS, WIN, WIN)
        mask_full = jnp.broadcast_to(mask_row[:, None], (level_win, lon_win, WIN, WIN)).reshape(level_win * lon_win, WIN, WIN)
        attn_out, grad_input, grad_wqkv, grad_wout, grad_logits = attend(input_row, grad_row, pos_bias, mask_full, w_qkv, w_out)
        summed = lax.optimization_barrier(jnp.sum(grad_logits.reshape(level_win, lon_win, HEADS, WIN, WIN), 1))
        return (attn_out, grad_input, grad_wqkv, grad_wout, table_grad(summed, index_table))
    attn_rows, grad_rows, wqkv_rows, wout_rows, table_parts = lax.map(one_row, (input_blocks, grad_blocks, table_rows, allowed))
    attn_rows = attn_rows.reshape(lat_win, level_win, lon_win, WIN, channels).transpose(1, 0, 2, 3, 4)
    grad_rows = grad_rows.reshape(lat_win, level_win, lon_win, WIN, channels).transpose(1, 0, 2, 3, 4)
    attn = jnp.roll(from_windows(attn_rows), returns, (0, 1, 2))
    outputs = (upcast(features) + upcast(attn)).astype(jnp.bfloat16)
    grad_normed = jnp.roll(from_windows(grad_rows), returns, (0, 1, 2))
    grad_features, grad_gain, grad_shift = norm_backward(grad_normed, x_hat, inv_std, norm_gain, cotangent)
    factor = TOKENS ** (-0.5)
    grad_wqkv = lax.optimization_barrier(jnp.sum(wqkv_rows, 0)) * factor
    grad_wout = lax.optimization_barrier(jnp.sum(wout_rows, 0)) * factor
    grad_table = table_parts.transpose(1, 0, 2, 3) * factor
    return (outputs, grad_features, grad_gain * factor, grad_shift * factor, grad_wqkv, grad_wout, grad_table)
```

```python
import functools

import jax
import jax.numpy as jnp
import numpy as np
from jax import lax
from jax.experimental import pallas as pl
from jax.experimental.pallas import tpu as pltpu
from jax.sharding import PartitionSpec as P

HEADS = 6
WZ = 2
WH = 6
WW = 12
BLOCK = WZ * WH
WIN = BLOCK * WW
SPANS = 2 * WW - 1
SPREAD = 384
LANES = 128
PAD_LON = 16
PAD_QUAD = 80
LARGE = 1e30

epsilon = 1e-05

f32, bf16 = jnp.float32, jnp.bfloat16


def call(body, outs, scratch=(), flops=0, moved=0, **kwargs):
    return pl.pallas_call(
        body,
        out_shape=outs,
        scratch_shapes=list(scratch),
        compiler_params=pltpu.CompilerParams(vmem_limit_bytes=48 * 1024 * 1024),
        cost_estimate=pl.CostEstimate(flops=flops, bytes_accessed=moved, transcendentals=0),
        **kwargs,
    )


def struct(shape, dtype):
    return jax.ShapeDtypeStruct(shape, dtype)


def quadrants(levels, lat_rows, lon_cols):
    lat_cut, lon_cut = WH // 2, WW // 2
    high_lat, low_lat = range(lat_cut, lat_rows), range(lat_cut)
    high_lon, low_lon = range(lon_cut, lon_cols), range(lon_cut)
    return (high_lat, high_lon), (high_lat, low_lon), (low_lat, high_lon), (low_lat, low_lon)


def pack_matrix(levels, lat_rows, lon_cols):
    picks = np.zeros((4 * PAD_QUAD, levels * lat_rows * PAD_LON), np.float32)
    for q, (rows, cols) in enumerate(quadrants(levels, lat_rows, lon_cols)):
        at = q * PAD_QUAD
        for z in range(levels):
            for a in rows:
                for o in cols:
                    picks[at, (z * lat_rows + a) * PAD_LON + o] = 1
                    at += 1
    return jnp.asarray(picks, bf16)


def window_matrix(levels, lat_rows, lon_cols):
    lat_cut, lon_cut, level_cut = WH // 2, WW // 2, WZ // 2
    picks = np.zeros((levels // WZ * WIN, 4 * PAD_QUAD), np.float32)
    for q, (rows, cols) in enumerate(quadrants(levels, lat_rows, lon_cols)):
        at = q * PAD_QUAD
        for z in range(levels):
            for a in rows:
                for o in cols:
                    level = (z - level_cut) % levels
                    lat = (a - lat_cut) % lat_rows
                    lon = (o - lon_cut) % lon_cols
                    token = lon * BLOCK + level % WZ * WH + lat
                    picks[level // WZ * WIN + token, at] = 1
                    at += 1
    return jnp.asarray(picks, bf16)


def spread_matrices():
    last, first = np.zeros((2, WIN, SPREAD), np.float32)
    for span in range(SPANS):
        for cell in range(BLOCK):
            if span < WW - 1:
                last[cell * WW + span, span * BLOCK + cell] = 1
            else:
                first[cell * WW + span - (WW - 1), span * BLOCK + cell] = 1
    return jnp.asarray(last, bf16), jnp.asarray(first, bf16)


def apart():
    cell = np.arange(16)[:, None] % BLOCK
    other = np.arange(SPREAD)[None, :] % BLOCK
    level = (cell // WH >= WZ // 2) != (other // WH >= WZ // 2)
    row = (cell % WH >= WH // 2) != (other % WH >= WH // 2)
    return jnp.asarray(level, f32), jnp.asarray(row, f32)


def pack_body(features, cotangent, picks, *outs):
    levels, lat_rows, lon_cols, width = features.shape
    for at, ref in enumerate((features, cotangent)):
        cells = ref[...].astype(f32)
        fill = jnp.zeros((levels, lat_rows, PAD_LON - lon_cols, width), f32)
        cells = jnp.concatenate((cells, fill), 2).reshape(levels * lat_rows * PAD_LON, width)
        packed = jnp.dot(picks[...], cells.astype(bf16), preferred_element_type=f32).astype(bf16)
        for q, out in enumerate(outs):
            out[:, at * width : (at + 1) * width] = packed[q * PAD_QUAD : (q + 1) * PAD_QUAD]


def unpack_body(here, from_lon, from_lat, from_both, picks, outputs, grad_features):
    levels, lat_rows, lon_cols, width = outputs.shape
    for at, ref in enumerate((outputs, grad_features)):
        part = slice(at * width, (at + 1) * width)
        quads = jnp.concatenate([q[:, part] for q in (here, from_lon, from_lat, from_both)], 0)
        cells = lax.dot_general(
            picks[...], quads, (((0,), (0,)), ((), ())), preferred_element_type=f32
        )
        ref[...] = cells.reshape(levels, lat_rows, PAD_LON, width)[:, :, :lon_cols].astype(bf16)


def spread_index(index_table, last, first):
    parts = []
    rows = [
        jnp.concatenate([index_table[c * WW + a : c * WW + a + 1, :] for c in range(BLOCK)], 0)
        for a in (WW - 1, 0)
    ]
    fill = jnp.zeros((16 - BLOCK, WIN), f32)
    for cut in (lambda v: v // LANES, lambda v: v % LANES):
        total = jnp.zeros((16, SPREAD), f32)
        for labels, picks in zip(rows, (last, first)):
            value = jnp.concatenate((cut(labels).astype(f32), fill), 0).astype(bf16)
            total += jnp.dot(value, picks[...], preferred_element_type=f32)
        parts.append(total.astype(jnp.int32))
    return parts


def bias_body(bias_table, index_table, last, first, level_apart, row_apart, out, chunk_out, lane_out, table):
    level_win, _, heads, labels = bias_table.shape
    chunk, lane = spread_index(index_table, last, first)
    chunk_out[...] = chunk
    lane_out[...] = lane
    chunks = -(-labels // LANES)
    for t in range(level_win):
        table[8 * t : 8 * t + heads, :labels] = bias_table[t, 0]
    top = lax.axis_index("lat") == lax.axis_size("lat") - 1
    barred_rows = jnp.logical_and(row_apart[...] > 0, top)
    for t in range(level_win):
        barred = barred_rows
        if t == level_win - 1:
            barred = jnp.logical_or(barred, level_apart[...] > 0)
        for h in range(heads):
            row = 8 * t + h
            tiles = []
            for tile in range(SPREAD // LANES):
                at = slice(tile * LANES, (tile + 1) * LANES)
                found = jnp.zeros((16, LANES), f32)
                for c in range(chunks):
                    source = jnp.broadcast_to(
                        table[row : row + 1, c * LANES : (c + 1) * LANES], (16, LANES)
                    )
                    taken = jnp.take_along_axis(source, lane[:, at], axis=1, mode="promise_in_bounds")
                    found = jnp.where(chunk[:, at] == c, taken, found)
                tiles.append(found)
            value = jnp.where(barred, -LARGE, jnp.concatenate(tiles, 1))
            for a in range(WW):
                shift = (WW - 1 - a) * BLOCK
                out[t * heads + h, a * BLOCK : (a + 1) * BLOCK, :] = value[
                    :BLOCK, shift : shift + WIN
                ]


def inverse_body(chunk, lane, chunk_out, lane_out):
    pieces = SPREAD // LANES
    labels = chunk_out.shape[0]
    valid = SPANS * BLOCK
    total = jnp.zeros((2 * labels, LANES), f32)
    wide = lax.broadcasted_iota(jnp.int32, (labels, SPREAD), 1)
    tall = lax.broadcasted_iota(jnp.int32, (labels, SPREAD), 0)
    lanes = lax.broadcasted_iota(jnp.int32, (LANES, SPREAD), 0)
    for cell in range(BLOCK):
        own = jnp.logical_and(chunk[cell : cell + 1, :] == tall, wide < valid)
        piece = jnp.where(own, (cell * pieces + wide // LANES).astype(f32), 0.0)
        spot = jnp.where(own, (wide % LANES).astype(f32), 0.0)
        both = jnp.concatenate((piece, spot), 0).astype(bf16)
        hit = jnp.where(lane[cell : cell + 1, :] == lanes, 1.0, 0.0).astype(bf16)
        total += lax.dot_general(both, hit, (((1,), (1,)), ((), ())), preferred_element_type=f32)
    chunk_out[...] = total[:labels].astype(jnp.int32)
    lane_out[...] = total[labels:].astype(jnp.int32)


def place_body(blocks, piece, spot, out):
    count, rows, _ = blocks.shape
    per = rows // BLOCK
    pieces = SPREAD // LANES
    chunks = piece.shape[0]
    at_piece = [jnp.broadcast_to(piece[c : c + 1, :], (8, LANES)) for c in range(out.shape[1] // LANES)]
    at_spot = [jnp.broadcast_to(spot[c : c + 1, :], (8, LANES)) for c in range(out.shape[1] // LANES)]
    found = [jnp.zeros((8, LANES), f32) for _ in at_piece]
    values = [blocks[b].astype(f32) for b in range(count)]
    for cell in range(BLOCK):
        for tile in range(pieces):
            source = jnp.concatenate(
                [
                    values[h // per * pieces + tile][h % per * BLOCK + cell : h % per * BLOCK + cell + 1]
                    for h in range(HEADS)
                ]
                + [jnp.zeros((8 - HEADS, LANES), f32)],
                0,
            )
            for c in range(len(found)):
                taken = jnp.take_along_axis(source, at_spot[c], axis=1, mode="promise_in_bounds")
                found[c] = jnp.where(at_piece[c] == cell * pieces + tile, taken, found[c])
    for c in range(len(found)):
        out[:, c * LANES : (c + 1) * LANES] = found[c].astype(bf16)


def window_body(
    here, from_lon, from_lat, from_both, picks, norm_gain, norm_shift, w_qkv, w_out, bias,
    out_here, out_lon, out_lat, out_both, keep, send, gathered, proj_grad, sums, tables,
):
    width = w_out.shape[0]
    level_win = bias.shape[0] // HEADS
    head_size = width // HEADS
    scaling = head_size ** (-0.5)
    quads = jnp.concatenate([q[...] for q in (here, from_lon, from_lat, from_both)], 0)
    features = jnp.dot(picks[...], quads[:, :width], preferred_element_type=f32)
    cotangent = jnp.dot(picks[...], quads[:, width:], preferred_element_type=f32)
    grad_shifted = cotangent.astype(bf16)
    gain = norm_gain[...]
    center = features - jnp.mean(features, -1, keepdims=True)
    inv_std = lax.rsqrt(jnp.mean(center * center, -1, keepdims=True) + epsilon)
    x_hat = center * inv_std
    normed = (x_hat * gain + norm_shift[...]).astype(bf16)
    query, key, value = (
        jnp.dot(normed, w_qkv[:, k * width : (k + 1) * width], preferred_element_type=f32).astype(bf16)
        for k in range(3)
    )
    grad_heads = lax.dot_general(
        grad_shifted, w_out[...], (((1,), (1,)), ((), ())), preferred_element_type=f32
    ).astype(bf16)
    head_of = lax.broadcasted_iota(jnp.int32, (1, width), 1) // head_size
    mixed_parts = []
    for t in range(level_win):
        rows = slice(t * WIN, (t + 1) * WIN)
        q, k, v, g = query[rows], key[rows], value[rows], grad_heads[rows]
        q_heads = [jnp.where(head_of == h, q, jnp.zeros_like(q)) for h in range(HEADS)]
        g_heads = [jnp.where(head_of == h, g, jnp.zeros_like(g)) for h in range(HEADS)]
        mixed = jnp.zeros((WIN, width), f32)
        grad_query = jnp.zeros((WIN, width), f32)
        grad_key = jnp.zeros((WIN, width), f32)
        grad_value = jnp.zeros((WIN, width), f32)
        for h in range(HEADS):
            logits = lax.dot_general(
                q_heads[h], k, (((1,), (1,)), ((), ())), preferred_element_type=f32
            )
            logits = logits * scaling + bias[t * HEADS + h]
            raised = jnp.exp(logits - jnp.max(logits, -1, keepdims=True))
            weights = raised * (1.0 / jnp.sum(raised, -1, keepdims=True))
            weights_bf = weights.astype(bf16)
            mixed = jnp.where(
                head_of == h, jnp.dot(weights_bf, v, preferred_element_type=f32), mixed
            )
            grad_weights = lax.dot_general(
                g_heads[h], v, (((1,), (1,)), ((), ())), preferred_element_type=f32
            )
            grad_value += lax.dot_general(
                weights_bf, g_heads[h], (((0,), (0,)), ((), ())), preferred_element_type=f32
            )
            grad_logits = weights * (
                grad_weights - jnp.sum(weights * grad_weights, -1, keepdims=True)
            )
            logit_bf = grad_logits.astype(bf16)
            grad_query = jnp.where(
                head_of == h, jnp.dot(logit_bf, k, preferred_element_type=f32), grad_query
            )
            grad_key += lax.dot_general(
                logit_bf, q_heads[h], (((0,), (0,)), ((), ())), preferred_element_type=f32
            )
            total = jnp.zeros((BLOCK, SPREAD), f32)
            for a in range(WW):
                shift = (WW - 1 - a) * BLOCK
                piece = grad_logits[a * BLOCK : (a + 1) * BLOCK]
                piece = jnp.concatenate((piece, jnp.zeros((BLOCK, SPREAD - WIN), f32)), 1)
                total += pltpu.roll(piece, shift, 1) if shift else piece
            for tile in range(SPREAD // LANES):
                tables[t, h, tile] = total[:, tile * LANES : (tile + 1) * LANES]
        mixed_parts.append(mixed.astype(bf16))
        proj_grad[rows, :width] = (grad_query * scaling).astype(bf16)
        proj_grad[rows, width : 2 * width] = (grad_key * scaling).astype(bf16)
        proj_grad[rows, 2 * width :] = grad_value.astype(bf16)
    mixed = jnp.concatenate(mixed_parts, 0)
    attn = jnp.dot(mixed, w_out[...], preferred_element_type=f32).astype(bf16)
    outputs = (features + attn.astype(f32)).astype(bf16)
    grad_proj = proj_grad[...]
    grad_input = lax.dot_general(
        grad_proj, w_qkv[...], (((1,), (1,)), ((), ())), preferred_element_type=f32
    )
    upstream = grad_input.astype(bf16).astype(f32)
    gain_part = jnp.sum(upstream * x_hat, 0, keepdims=True)
    shift_part = jnp.sum(upstream, 0, keepdims=True)
    g_hat = upstream * gain
    centred = (
        g_hat
        - jnp.mean(g_hat, -1, keepdims=True)
        - x_hat * jnp.mean(g_hat * x_hat, -1, keepdims=True)
    )
    grad_features = (cotangent + inv_std * centred).astype(bf16)
    for at, result in enumerate((outputs, grad_features)):
        back = lax.dot_general(
            picks[...], result, (((0,), (0,)), ((), ())), preferred_element_type=f32
        ).astype(bf16)
        for q, out in enumerate((out_here, out_lon, out_lat, out_both)):
            out[:, at * width : (at + 1) * width] = back[q * PAD_QUAD : (q + 1) * PAD_QUAD]
    sums[:, : 3 * width] = lax.dot_general(
        normed, grad_proj, (((0,), (0,)), ((), ())), preferred_element_type=f32
    )
    sums[:, 3 * width :] = lax.dot_general(
        mixed, grad_shifted, (((0,), (0,)), ((), ())), preferred_element_type=f32
    )
    chunks, blocks, size, _ = gathered.shape
    lat_count = chunks // 2
    edge = jnp.zeros((size - 4, LANES), f32)
    fill = jnp.zeros((1, 2 * LANES - width), f32)
    ends = [gain_part[:, :LANES], jnp.concatenate((gain_part[:, LANES:], fill), 1)]
    ends += [shift_part[:, :LANES], jnp.concatenate((shift_part[:, LANES:], fill), 1)]
    ends = jnp.concatenate(ends + [edge], 0).astype(bf16)
    for j in range(chunks):
        for b in range(blocks - 1):
            gathered[j, b] = sums[
                j * size : (j + 1) * size, b * LANES : (b + 1) * LANES
            ].astype(bf16)
        gathered[j, blocks - 1] = ends
    core = lax.axis_index("lon") % 2
    lat = lax.axis_index("lat")
    per = size // BLOCK
    for half, out in enumerate((keep, send)):
        side = core ^ half
        for at in range(lat_count):
            out[at * blocks : (at + 1) * blocks] = gathered[side * lat_count + (lat ^ at)]
        for h in range(0, HEADS, per):
            for tile in range(SPREAD // LANES):
                block = jnp.concatenate([tables[side, h + i, tile] for i in range(per)], 0)
                out[lat_count * blocks + h // per * (SPREAD // LANES) + tile] = block.astype(bf16)


def tree(values):
    while len(values) > 1:
        values = [a + b for a, b in zip(values[::2], values[1::2])]
    return values[0]


def halves_body(keep, came, *outs):
    at = 0
    for out in outs:
        count = out.shape[0]
        part = slice(at, at + count)
        out[...] = (keep[part].astype(f32) + came[part].astype(f32)).astype(bf16)
        at += count


def lats_body(*refs):
    *pieces, tail, out = refs
    blocks = pieces[0].shape[0]
    out[:blocks] = tree([p[...].astype(f32) for p in pieces]).astype(bf16)
    out[blocks:] = tail[...]


def lons_body(count, *refs):
    pieces, (weights, tail) = refs[:count], refs[count:]
    blocks = weights.shape[0]
    total = tree([p[...].astype(f32) for p in pieces]).astype(bf16)
    weights[...] = total[:blocks]
    tail[...] = total[blocks:]


def finish_body(lat_count, factor, *refs):
    near, far = refs[:lat_count], refs[lat_count : 2 * lat_count]
    table_near, table_far, grad_gain, grad_shift, grad_wqkv, grad_wout, grad_table, chunks, halves = refs[
        2 * lat_count :
    ]
    core = lax.axis_index("lon") % 2
    lat = lax.axis_index("lat")
    _, blocks, size, _ = chunks.shape
    for half, group in enumerate((near, far)):
        for at, ref in enumerate(group):
            chunks[(core ^ half) * lat_count + (lat ^ at)] = ref[...].astype(f32) * factor
    halves[core] = table_near[...].astype(f32) * factor
    halves[core ^ 1] = table_far[...].astype(f32) * factor
    width = grad_wout.shape[0]
    for j in range(chunks.shape[0]):
        rows = slice(j * size, (j + 1) * size)
        whole = jnp.concatenate([chunks[j, b] for b in range(blocks - 1)], 1)
        grad_wqkv[rows, :] = whole[:, : 3 * width]
        grad_wout[rows, :] = whole[:, 3 * width :]
    rest = width - LANES
    for at, out in enumerate((grad_gain, grad_shift)):
        out[:, :LANES] = chunks[0, blocks - 1, 2 * at : 2 * at + 1]
        out[:, LANES:] = chunks[0, blocks - 1, 2 * at + 1 : 2 * at + 2, :rest]
    for t in range(grad_table.shape[0]):
        grad_table[t, 0] = halves[t, : grad_table.shape[2], : grad_table.shape[3]]


def swap(value, axis, distance):
    count = lax.axis_size(axis)
    return lax.ppermute(value, axis, [(source, source ^ distance) for source in range(count)])


def send_back(value, lat_step, lon_step):
    lat_count, lon_count = lax.axis_size("lat"), lax.axis_size("lon")
    pairs = [
        (r * lon_count + c, (r + lat_step) % lat_count * lon_count + (c + lon_step) % lon_count)
        for r in range(lat_count)
        for c in range(lon_count)
    ]
    return lax.ppermute(value, ("lat", "lon"), pairs)


def on_device(features, norm_gain, norm_shift, w_qkv, w_out, bias_table, index_table, cotangent):
    levels, lat_rows, lon_cols, width = features.shape
    level_win, _, heads, labels = bias_table.shape
    lat_count, lon_count = lax.axis_size("lat"), lax.axis_size("lon")
    grid = (levels, lat_rows, lon_cols)
    to_quads, to_windows = pack_matrix(*grid), window_matrix(*grid)
    quad = struct((PAD_QUAD, 2 * width), bf16)
    steps = ((0, 1), (1, 0), (1, 1))

    here, *edges = call(pack_body, (quad,) * 4)(features, cotangent, to_quads)
    came = [send_back(e, -lat, -lon) for e, (lat, lon) in zip(edges, steps)]

    spread = struct((16, SPREAD), jnp.int32)
    bias, chunk, lane = call(
        bias_body,
        (struct((level_win * heads, WIN, WIN), f32), spread, spread),
        [pltpu.VMEM((8 * level_win, -(-labels // LANES) * LANES), f32)],
        moved=4 * 10**6,
    )(bias_table, index_table, *spread_matrices(), *apart())

    size = width // (2 * lat_count)
    blocks = 4 * width // LANES + 1
    table_blocks = HEADS * BLOCK * SPREAD // (size * LANES)
    half = struct((lat_count * blocks + table_blocks, size, LANES), bf16)
    out_here, *backs, keep, send = call(
        window_body,
        (quad,) * 4 + (half, half),
        [
            pltpu.VMEM((2 * lat_count, blocks, size, LANES), bf16),
            pltpu.VMEM((level_win * WIN, 3 * width), bf16),
            pltpu.VMEM((width, 4 * width), f32),
            pltpu.VMEM((level_win, heads, SPREAD // LANES, BLOCK, LANES), f32),
        ],
    )(here, *came, to_windows, norm_gain[None], norm_shift[None], w_qkv, w_out, bias)

    returned = [send_back(b, lat, lon) for b, (lat, lon) in zip(backs, steps)]

    chunk_shape = struct((blocks, size, LANES), bf16)
    tail_shape = struct((table_blocks, size, LANES), bf16)
    *pieces, tail = call(halves_body, (chunk_shape,) * lat_count + (tail_shape,))(
        keep, swap(send, "lon", 1)
    )
    pieces = pieces[:1] + [swap(p, "lat", at + 1) for at, p in enumerate(pieces[1:])]
    part = call(lats_body, struct((blocks + table_blocks, size, LANES), bf16))(*pieces, tail)
    parts = [part] + [swap(part, "lon", 2 * at) for at in range(1, lon_count // 2)]
    weights, tail = call(functools.partial(lons_body, len(parts)), (chunk_shape, tail_shape))(*parts)
    near = [weights] + [swap(weights, "lat", at) for at in range(1, lat_count)]

    places = struct((32, LANES), jnp.int32)
    piece, spot = call(inverse_body, (places, places))(chunk, lane)
    table_near = call(place_body, struct((8, -(-labels // LANES) * LANES), bf16))(tail, piece, spot)
    table_far = swap(table_near, "lon", 1)
    far = [swap(n, "lon", 1) for n in near]

    outputs, grad_features = call(unpack_body, (struct(features.shape, bf16),) * 2)(
        out_here, *returned, to_quads
    )
    factor = (levels * lat_rows * lat_count * lon_cols * lon_count) ** (-0.5)
    row = struct((1, width), f32)
    grad_gain, grad_shift, grad_wqkv, grad_wout, grad_table = call(
        functools.partial(finish_body, lat_count, factor),
        (row, row, struct(w_qkv.shape, f32), struct(w_out.shape, f32), struct(bias_table.shape, f32)),
        [
            pltpu.VMEM((2 * lat_count, blocks, size, LANES), f32),
            pltpu.VMEM((2,) + table_near.shape, f32),
        ],
    )(*near, *far, table_near, table_far)
    return (
        outputs,
        grad_features,
        grad_gain[0],
        grad_shift[0],
        grad_wqkv,
        grad_wout,
        grad_table,
    )


def solution(mesh):
    placed = (
        P(None, "lat", "lon", None),
        P(),
        P(),
        P(),
        P(),
        P(None, "lat", None, None),
        P(),
        P(None, "lat", "lon", None),
    )
    return jax.shard_map(
        on_device,
        mesh=mesh,
        in_specs=placed,
        out_specs=(
            P(None, "lat", "lon", None),
            P(None, "lat", "lon", None),
            P(),
            P(),
            P(),
            P(),
            P(None, "lat", None, None),
        ),
        check_vma=False,
    )
```

```python
import functools

import jax
import jax.numpy as jnp
from jax import lax
from jax.experimental import pallas as pl
from jax.experimental.pallas import tpu as pltpu
from jax.sharding import PartitionSpec as P

HEADS = 6
WZ = 2
WH = 6
WW = 12
BLOCK = WZ * WH
WIN = BLOCK * WW
SPANS = 2 * WW - 1
SPREAD = 384
LANES = 128
PAD_LEVEL = 8
LARGE = 1e30

epsilon = 1e-05

f32, bf16 = jnp.float32, jnp.bfloat16


def call(body, outs, scratch=(), flops=0, moved=0, **kwargs):
    return pl.pallas_call(
        body,
        out_shape=outs,
        scratch_shapes=list(scratch),
        compiler_params=pltpu.CompilerParams(vmem_limit_bytes=48 * 1024 * 1024),
        cost_estimate=pl.CostEstimate(flops=flops, bytes_accessed=moved, transcendentals=0),
        **kwargs,
    )


def struct(shape, dtype):
    return jax.ShapeDtypeStruct(shape, dtype)


def quotient(value, divisor):
    return (value * (65536 // divisor + 1)) >> 16


def columns(shape, dim):
    return lax.broadcasted_iota(jnp.int32, shape, dim)


def hot(condition):
    return jnp.where(condition, 1.0, 0.0).astype(bf16)


def quadrants(lat_rows, lon_cols):
    lat_cut, lon_cut = WH // 2, WW // 2
    high_lat, low_lat = slice(lat_cut, lat_rows), slice(lat_cut)
    high_lon, low_lon = slice(lon_cut, lon_cols), slice(lon_cut)
    return (high_lat, high_lon), (high_lat, low_lon), (low_lat, high_lon), (low_lat, low_lon)


def window_matrix(levels, room):
    lat_cut, lon_cut, level_cut = WH // 2, WW // 2, WZ // 2
    count = levels // WZ * WIN
    token = columns((count, 1), 0)
    window = quotient(token, WIN)
    inside = token - window * WIN
    lon = quotient(inside, BLOCK)
    cell = inside - lon * BLOCK
    depth = quotient(cell, WH)
    lat = cell - depth * WH
    level = window * WZ + depth + level_cut
    level = jnp.where(level >= levels, level - levels, level)
    late_lon, late_lat = lon >= lon_cut, lat >= lat_cut
    quad = jnp.where(late_lat, 2, 0) + jnp.where(late_lon, 1, 0)
    row = jnp.where(late_lat, lat - lat_cut, lat)
    col = jnp.where(late_lon, lon - lon_cut, lon)
    source = ((quad * lat_cut + row) * lon_cut + col) * room + level
    return hot(columns((count, WIN // WZ * room), 1) == source)


def pack_body(count, *refs):
    features, cotangent, *plain = refs[: count + 2]
    *outs, sems = refs[count + 2 :]
    lat_rows, lon_cols, _, _ = features.shape
    pairs = []
    for (rows, cols), out in zip(quadrants(lat_rows, lon_cols), outs):
        pairs += [(features.at[rows, cols], out.at[0]), (cotangent.at[rows, cols], out.at[1])]
    pairs += zip(plain, outs[4:])
    copies = [pltpu.make_async_copy(*pair, sems.at[at]) for at, pair in enumerate(pairs)]
    for copy in copies:
        copy.start()
    for copy in copies:
        copy.wait()


def unpack_body(here, lat_piece, lon_pair, outputs, grad_features):
    lat_rows, lon_cols, levels, width = outputs.shape
    blocks = here.shape[0]
    start = lat_piece.shape[0] - 2 * blocks
    quads = (
        here[...],
        lon_pair[:blocks],
        lat_piece[start : start + blocks],
        lon_pair[blocks:],
    )
    for (rows, cols), quad in zip(quadrants(lat_rows, lon_cols), quads):
        tiles = quad.astype(f32).reshape(3, -1, LANES)
        rest = width - LANES
        pair = (
            jnp.concatenate((tiles[0], tiles[2][:, :rest]), 1),
            jnp.concatenate((tiles[1], tiles[2][:, rest:]), 1),
        )
        for value, out in zip(pair, (outputs, grad_features)):
            value = value.reshape(WH // 2, WW // 2, levels, width)
            out[rows, cols] = value.astype(bf16)


def spread_index(index_table):
    parts = []
    rows = [
        jnp.concatenate([index_table[c * WW + a : c * WW + a + 1, :] for c in range(BLOCK)], 0)
        for a in (WW - 1, 0)
    ]
    fill = jnp.zeros((16 - BLOCK, WIN), f32)
    token = columns((WIN, 1), 0)
    cell = quotient(token, WW)
    entry = (token - cell * WW) * BLOCK + cell
    wide = columns((WIN, SPREAD), 1)
    cut_at = (WW - 1) * BLOCK
    picks = (
        hot(jnp.logical_and(entry == wide, wide < cut_at)),
        hot(entry + cut_at == wide),
    )
    for cut in (lambda v: v >> 7, lambda v: v & (LANES - 1)):
        total = jnp.zeros((16, SPREAD), f32)
        for labels, pick in zip(rows, picks):
            value = jnp.concatenate((cut(labels).astype(f32), fill), 0).astype(bf16)
            total += jnp.dot(value, pick, preferred_element_type=f32)
        parts.append(total.astype(jnp.int32))
    return parts


def bias_body(bias_table, index_table, out, chunk_out, lane_out, table):
    level_win, heads, _, labels = bias_table.shape
    chunk, lane = spread_index(index_table)
    chunk_out[...] = chunk
    lane_out[...] = lane
    chunks = -(-labels // LANES)
    for t in range(level_win):
        for h in range(heads):
            table[t * heads + h : t * heads + h + 1, :labels] = bias_table[t, h]
    cell = columns((16, 1), 0)
    other = columns((1, SPREAD), 1)
    other = other - quotient(other, BLOCK) * BLOCK
    level_apart = (cell >= WH) != (other >= WH)
    cell = jnp.where(cell >= WH, cell - WH, cell)
    other = jnp.where(other >= WH, other - WH, other)
    row_apart = (cell >= WH // 2) != (other >= WH // 2)
    top = lax.axis_index("lat") == lax.axis_size("lat") - 1
    barred_rows = jnp.logical_and(row_apart, top)
    for t in range(level_win):
        barred = barred_rows
        if t == level_win - 1:
            barred = jnp.logical_or(barred, level_apart)
        for h in range(heads):
            row = t * heads + h
            tiles = []
            for tile in range(SPREAD // LANES):
                at = slice(tile * LANES, (tile + 1) * LANES)
                found = jnp.zeros((16, LANES), f32)
                for c in range(chunks):
                    source = jnp.broadcast_to(
                        table[row : row + 1, c * LANES : (c + 1) * LANES], (16, LANES)
                    )
                    taken = jnp.take_along_axis(source, lane[:, at], axis=1, mode="promise_in_bounds")
                    found = jnp.where(chunk[:, at] == c, taken, found)
                tiles.append(found)
            value = jnp.where(barred, -LARGE, jnp.concatenate(tiles, 1))
            for a in range(WW):
                shift = (WW - 1 - a) * BLOCK
                out[row, a * BLOCK : (a + 1) * BLOCK, :] = value[:BLOCK, shift : shift + WIN]


def inverse_body(chunk, lane, chunk_out, lane_out):
    pieces = SPREAD // LANES
    labels = chunk_out.shape[0]
    valid = SPANS * BLOCK
    total = jnp.zeros((2 * labels, LANES), f32)
    wide = lax.broadcasted_iota(jnp.int32, (labels, SPREAD), 1)
    tall = lax.broadcasted_iota(jnp.int32, (labels, SPREAD), 0)
    lanes = lax.broadcasted_iota(jnp.int32, (LANES, SPREAD), 0)
    for cell in range(BLOCK):
        own = jnp.logical_and(chunk[cell : cell + 1, :] == tall, wide < valid)
        piece = jnp.where(own, (cell * pieces + wide // LANES).astype(f32), 0.0)
        spot = jnp.where(own, (wide % LANES).astype(f32), 0.0)
        both = jnp.concatenate((piece, spot), 0).astype(bf16)
        hit = jnp.where(lane[cell : cell + 1, :] == lanes, 1.0, 0.0).astype(bf16)
        total += lax.dot_general(both, hit, (((1,), (1,)), ((), ())), preferred_element_type=f32)
    chunk_out[...] = total[:labels].astype(jnp.int32)
    lane_out[...] = total[labels:].astype(jnp.int32)


def place_body(blocks, piece, spot, out):
    count, rows, _ = blocks.shape
    per = rows // BLOCK
    pieces = SPREAD // LANES
    chunks = piece.shape[0]
    at_piece = [jnp.broadcast_to(piece[c : c + 1, :], (8, LANES)) for c in range(out.shape[1] // LANES)]
    at_spot = [jnp.broadcast_to(spot[c : c + 1, :], (8, LANES)) for c in range(out.shape[1] // LANES)]
    found = [jnp.zeros((8, LANES), f32) for _ in at_piece]
    values = [blocks[b].astype(f32) for b in range(count)]
    for cell in range(BLOCK):
        for tile in range(pieces):
            source = jnp.concatenate(
                [
                    values[h // per * pieces + tile][h % per * BLOCK + cell : h % per * BLOCK + cell + 1]
                    for h in range(HEADS)
                ]
                + [jnp.zeros((8 - HEADS, LANES), f32)],
                0,
            )
            for c in range(len(found)):
                taken = jnp.take_along_axis(source, at_spot[c], axis=1, mode="promise_in_bounds")
                found[c] = jnp.where(at_piece[c] == cell * pieces + tile, taken, found[c])
    for c in range(len(found)):
        out[:, c * LANES : (c + 1) * LANES] = found[c].astype(bf16)


def window_body(
    here, from_lon, from_lat, from_both, norm_gain, norm_shift, w_qkv, w_out, bias,
    out_here, out_lon, out_lat, keep, send, gathered, proj_grad, sums, tables,
):
    width = w_out.shape[0]
    level_win = bias.shape[0] // HEADS
    head_size = width // HEADS
    scaling = head_size ** (-0.5)
    _, lat_half, lon_half, levels, _ = here.shape
    quad_rows = lat_half * lon_half * PAD_LEVEL
    fill = jnp.zeros((lat_half, lon_half, PAD_LEVEL - levels, width), f32)
    picks = window_matrix(levels, PAD_LEVEL)
    features, cotangent = (
        jnp.dot(
            picks,
            jnp.concatenate(
                [
                    jnp.concatenate((quad[at].astype(f32), fill), 2).reshape(quad_rows, width)
                    for quad in (here, from_lon, from_lat, from_both)
                ],
                0,
            ).astype(bf16),
            preferred_element_type=f32,
        )
        for at in range(2)
    )
    grad_shifted = cotangent.astype(bf16)
    gain = norm_gain[...]
    center = features - jnp.mean(features, -1, keepdims=True)
    inv_std = lax.rsqrt(jnp.mean(center * center, -1, keepdims=True) + epsilon)
    x_hat = center * inv_std
    normed = (x_hat * gain + norm_shift[...]).astype(bf16)
    query, key, value = (
        jnp.dot(normed, w_qkv[:, k * width : (k + 1) * width], preferred_element_type=f32).astype(bf16)
        for k in range(3)
    )
    grad_heads = lax.dot_general(
        grad_shifted, w_out[...], (((1,), (1,)), ((), ())), preferred_element_type=f32
    ).astype(bf16)
    head_of = lax.broadcasted_iota(jnp.int32, (1, width), 1) // head_size
    mixed_parts = []
    for t in range(level_win):
        rows = slice(t * WIN, (t + 1) * WIN)
        q, k, v, g = query[rows], key[rows], value[rows], grad_heads[rows]
        q_heads = [jnp.where(head_of == h, q, jnp.zeros_like(q)) for h in range(HEADS)]
        g_heads = [jnp.where(head_of == h, g, jnp.zeros_like(g)) for h in range(HEADS)]
        mixed = jnp.zeros((WIN, width), f32)
        grad_query = jnp.zeros((WIN, width), f32)
        grad_key = jnp.zeros((WIN, width), f32)
        grad_value = jnp.zeros((WIN, width), f32)
        for h in range(HEADS):
            logits = lax.dot_general(
                q_heads[h], k, (((1,), (1,)), ((), ())), preferred_element_type=f32
            )
            logits = logits * scaling + bias[t * HEADS + h]
            raised = jnp.exp(logits - jnp.max(logits, -1, keepdims=True))
            weights = raised * (1.0 / jnp.sum(raised, -1, keepdims=True))
            weights_bf = weights.astype(bf16)
            mixed = jnp.where(
                head_of == h, jnp.dot(weights_bf, v, preferred_element_type=f32), mixed
            )
            grad_weights = lax.dot_general(
                g_heads[h], v, (((1,), (1,)), ((), ())), preferred_element_type=f32
            )
            grad_value += lax.dot_general(
                weights_bf, g_heads[h], (((0,), (0,)), ((), ())), preferred_element_type=f32
            )
            grad_logits = weights * (
                grad_weights - jnp.sum(weights * grad_weights, -1, keepdims=True)
            )
            logit_bf = grad_logits.astype(bf16)
            grad_query = jnp.where(
                head_of == h, jnp.dot(logit_bf, k, preferred_element_type=f32), grad_query
            )
            grad_key += lax.dot_general(
                logit_bf, q_heads[h], (((0,), (0,)), ((), ())), preferred_element_type=f32
            )
            total = jnp.zeros((BLOCK, SPREAD), f32)
            for a in range(WW):
                shift = (WW - 1 - a) * BLOCK
                piece = grad_logits[a * BLOCK : (a + 1) * BLOCK]
                piece = jnp.concatenate((piece, jnp.zeros((BLOCK, SPREAD - WIN), f32)), 1)
                total += pltpu.roll(piece, shift, 1) if shift else piece
            for tile in range(SPREAD // LANES):
                tables[t, h, tile] = total[:, tile * LANES : (tile + 1) * LANES]
        mixed_parts.append(mixed.astype(bf16))
        proj_grad[rows, :width] = (grad_query * scaling).astype(bf16)
        proj_grad[rows, width : 2 * width] = (grad_key * scaling).astype(bf16)
        proj_grad[rows, 2 * width :] = grad_value.astype(bf16)
    mixed = jnp.concatenate(mixed_parts, 0)
    attn = jnp.dot(mixed, w_out[...], preferred_element_type=f32).astype(bf16)
    outputs = (features + attn.astype(f32)).astype(bf16)
    grad_proj = proj_grad[...]
    grad_input = lax.dot_general(
        grad_proj, w_qkv[...], (((1,), (1,)), ((), ())), preferred_element_type=f32
    )
    upstream = grad_input.astype(bf16).astype(f32)
    gain_part = jnp.sum(upstream * x_hat, 0, keepdims=True)
    shift_part = jnp.sum(upstream, 0, keepdims=True)
    g_hat = upstream * gain
    centred = (
        g_hat
        - jnp.mean(g_hat, -1, keepdims=True)
        - x_hat * jnp.mean(g_hat * x_hat, -1, keepdims=True)
    )
    grad_features = (cotangent + inv_std * centred).astype(bf16)
    picks = window_matrix(levels, levels)
    back = [
        lax.dot_general(picks, result, (((0,), (0,)), ((), ())), preferred_element_type=f32)
        for result in (outputs, grad_features)
    ]
    rest = width - LANES
    tiles = [b[:, :LANES] for b in back]
    tiles.append(jnp.concatenate([b[:, LANES:] for b in back], 1))
    size = gathered.shape[2]
    groups = lat_half * lon_half * levels // size
    for at, tile in enumerate(tiles):
        for q, (out, first) in enumerate(
            ((out_here, 0), (out_lon, 0), (out_lat, 0), (out_lat, 3 * groups))
        ):
            for i in range(groups):
                row = (q * groups + i) * size
                out[first + at * groups + i] = tile[row : row + size].astype(bf16)
    sums[:, : 3 * width] = lax.dot_general(
        normed, grad_proj, (((0,), (0,)), ((), ())), preferred_element_type=f32
    )
    sums[:, 3 * width :] = lax.dot_general(
        mixed, grad_shifted, (((0,), (0,)), ((), ())), preferred_element_type=f32
    )
    chunks, blocks, _, _ = gathered.shape
    lat_count = chunks // 2
    edge = jnp.zeros((size - 4, LANES), f32)
    fill = jnp.zeros((1, 2 * LANES - width), f32)
    ends = [gain_part[:, :LANES], jnp.concatenate((gain_part[:, LANES:], fill), 1)]
    ends += [shift_part[:, :LANES], jnp.concatenate((shift_part[:, LANES:], fill), 1)]
    ends = jnp.concatenate(ends + [edge], 0).astype(bf16)
    for j in range(chunks):
        for b in range(blocks - 1):
            gathered[j, b] = sums[
                j * size : (j + 1) * size, b * LANES : (b + 1) * LANES
            ].astype(bf16)
        gathered[j, blocks - 1] = ends
    core = lax.axis_index("lon") % 2
    lat = lax.axis_index("lat")
    per = size // BLOCK
    for half, out in enumerate((keep, send)):
        side = core ^ half
        for at in range(lat_count):
            out[at * blocks : (at + 1) * blocks] = gathered[
                side * lat_count + lax.rem(lat + at, lat_count)
            ]
        for h in range(0, HEADS, per):
            for tile in range(SPREAD // LANES):
                block = jnp.concatenate([tables[side, h + i, tile] for i in range(per)], 0)
                out[lat_count * blocks + h // per * (SPREAD // LANES) + tile] = block.astype(bf16)


def tree(values):
    while len(values) > 1:
        values = [a + b for a, b in zip(values[::2], values[1::2])]
    return values[0]


def halves_body(keep, came, quads, *outs):
    *pieces, tail = outs
    blocks = pieces[0].shape[0]
    at = 0
    for out in outs:
        count = tail.shape[0] if out is tail else blocks
        part = slice(at, at + count)
        out[:count] = (keep[part].astype(f32) + came[part].astype(f32)).astype(bf16)
        at += count
    pieces[1][blocks:] = quads[...]


def lats_body(*refs):
    *pieces, tail, quad, out, onward = refs
    blocks = pieces[0].shape[0]
    out[:blocks] = tree([p[:blocks].astype(f32) for p in pieces]).astype(bf16)
    out[blocks:] = tail[...]
    count = quad.shape[0]
    onward[:count] = quad[...]
    onward[count:] = pieces[1][blocks + count :]


def lons_body(count, *refs):
    pieces, (weights, tail) = refs[:count], refs[count:]
    blocks = weights.shape[0]
    total = tree([p[...].astype(f32) for p in pieces]).astype(bf16)
    weights[...] = total[:blocks]
    tail[...] = total[blocks:]


def finish_body(lat_count, factor, *refs):
    near, far = refs[:lat_count], refs[lat_count : 2 * lat_count]
    table_near, table_far, grad_gain, grad_shift, grad_wqkv, grad_wout, grad_table, chunks, halves = refs[
        2 * lat_count :
    ]
    core = lax.axis_index("lon") % 2
    lat = lax.axis_index("lat")
    _, blocks, size, _ = chunks.shape
    for half, group in enumerate((near, far)):
        for at, ref in enumerate(group):
            chunks[(core ^ half) * lat_count + lax.rem(lat + lat_count - at, lat_count)] = ref[...].astype(f32) * factor
    halves[core] = table_near[...].astype(f32) * factor
    halves[core ^ 1] = table_far[...].astype(f32) * factor
    width = grad_wout.shape[0]
    for j in range(chunks.shape[0]):
        rows = slice(j * size, (j + 1) * size)
        whole = jnp.concatenate([chunks[j, b] for b in range(blocks - 1)], 1)
        grad_wqkv[rows, :] = whole[:, : 3 * width]
        grad_wout[rows, :] = whole[:, 3 * width :]
    rest = width - LANES
    for at, out in enumerate((grad_gain, grad_shift)):
        out[:, :LANES] = chunks[0, blocks - 1, 2 * at : 2 * at + 1]
        out[:, LANES:] = chunks[0, blocks - 1, 2 * at + 1 : 2 * at + 2, :rest]
    level_win, heads, _, labels = grad_table.shape
    for t in range(level_win):
        for h in range(heads):
            grad_table[t, h] = halves[t, h : h + 1, :labels]


def swap(value, axis, distance):
    count = lax.axis_size(axis)
    return lax.ppermute(value, axis, [(source, source ^ distance) for source in range(count)])


def shifted(value, lat_step, lon_step):
    lat_count, lon_count = lax.axis_size("lat"), lax.axis_size("lon")
    pairs = [
        (r * lon_count + c, (r + lat_step) % lat_count * lon_count + (c + lon_step) % lon_count)
        for r in range(lat_count)
        for c in range(lon_count)
    ]
    return lax.ppermute(value, ("lat", "lon"), pairs)


def on_device(features, norm_gain, norm_shift, w_qkv, w_out, bias_table, index_table, cotangent):
    levels, lat_rows, lon_cols, width = features.shape
    level_win, _, heads, labels = bias_table.shape
    lat_count, lon_count = lax.axis_size("lat"), lax.axis_size("lon")
    quad = struct((2, WH // 2, WW // 2, levels, width), bf16)
    steps = ((0, 1), (1, 0), (1, 1))

    plain = (
        norm_gain[None], norm_shift[None], w_qkv, w_out, bias_table.transpose(0, 2, 1, 3), index_table
    )
    far_side = pl.BlockSpec(memory_space=pltpu.HBM)
    *packed, gain, shift, w_qkv, w_out, table, labels_of = call(
        functools.partial(pack_body, len(plain)),
        (quad,) * 4 + tuple(struct(p.shape, p.dtype) for p in plain),
        [pltpu.SemaphoreType.DMA((8 + len(plain),))],
        in_specs=[far_side] * (2 + len(plain)),
    )(
        *(
            pltpu.with_memory_space_constraint(v, pltpu.HBM)
            for v in (features.transpose(1, 2, 0, 3), cotangent.transpose(1, 2, 0, 3), *plain)
        )
    )
    here, *edges = packed
    came = [shifted(e, -lat, -lon) for e, (lat, lon) in zip(edges, steps)]

    spread = struct((16, SPREAD), jnp.int32)
    whole_lanes = -(-labels // LANES) * LANES
    bias, chunk, lane = call(
        bias_body,
        (struct((level_win * heads, WIN, WIN), f32), spread, spread),
        [pltpu.VMEM((level_win * heads, whole_lanes), f32)],
        moved=16 * 10**6,
    )(table, labels_of)

    size = width // (2 * lat_count)
    blocks = 4 * width // LANES + 1
    table_blocks = HEADS * BLOCK * SPREAD // (size * LANES)
    quad_blocks = 2 * WH // 2 * WW // 2 * levels * width // (size * LANES)

    def stack(count):
        return struct((count, size, LANES), bf16)

    half = stack(lat_count * blocks + table_blocks)
    out_here, out_lon, out_lat, keep, send = call(
        window_body,
        (stack(quad_blocks), stack(quad_blocks), stack(2 * quad_blocks), half, half),
        [
            pltpu.VMEM((2 * lat_count, blocks, size, LANES), bf16),
            pltpu.VMEM((level_win * WIN, 3 * width), bf16),
            pltpu.VMEM((width, 4 * width), f32),
            pltpu.VMEM((level_win, heads, SPREAD // LANES, BLOCK, LANES), f32),
        ],
        moved=25 * 10**6,
    )(here, *came, gain, shift, w_qkv, w_out, bias)

    shapes = [stack(blocks)] * lat_count + [stack(table_blocks)]
    shapes[1] = stack(blocks + 2 * quad_blocks)
    *pieces, tail = call(halves_body, tuple(shapes))(keep, swap(send, "lon", 1), out_lat)
    pieces = [shifted(p, at, 0) if at else p for at, p in enumerate(pieces)]
    part, onward = call(lats_body, (stack(blocks + table_blocks), stack(2 * quad_blocks)))(
        *pieces, tail, out_lon
    )
    parts = [part] + [swap(part, "lon", 2 * at) for at in range(1, lon_count // 2)]
    lon_pair = shifted(onward, 0, 1)
    part, chunk, lane = lax.optimization_barrier((part, chunk, lane))
    places = struct((32, LANES), jnp.int32)
    piece, spot = call(inverse_body, (places, places), moved=2 * 10**6)(chunk, lane)
    weights, tail = call(functools.partial(lons_body, len(parts)), (stack(blocks), stack(table_blocks)))(
        *parts
    )
    near = [weights] + [shifted(weights, at, 0) for at in range(1, lat_count)]
    table_near = call(place_body, struct((8, whole_lanes), bf16), moved=5 * 10**6)(tail, piece, spot)
    table_far = swap(table_near, "lon", 1)
    far = [swap(n, "lon", 1) for n in near]

    cells = struct((lat_rows, lon_cols, levels, width), bf16)
    outputs, grad_features = call(unpack_body, (cells, cells), moved=2 * 10**6)(
        out_here, pieces[1], lon_pair
    )
    factor = (levels * lat_rows * lat_count * lon_cols * lon_count) ** (-0.5)
    row = struct((1, width), f32)
    grad_gain, grad_shift, grad_wqkv, grad_wout, grad_table = call(
        functools.partial(finish_body, lat_count, factor),
        (
            row,
            row,
            struct(w_qkv.shape, f32),
            struct(w_out.shape, f32),
            struct((level_win, heads, 1, labels), f32),
        ),
        [
            pltpu.VMEM((2 * lat_count, blocks, size, LANES), f32),
            pltpu.VMEM((2,) + table_near.shape, f32),
        ],
    )(*near, *far, table_near, table_far)
    return (
        outputs.transpose(2, 0, 1, 3),
        grad_features.transpose(2, 0, 1, 3),
        grad_gain[0],
        grad_shift[0],
        grad_wqkv,
        grad_wout,
        grad_table.transpose(0, 2, 1, 3),
    )


def solution(mesh):
    placed = (
        P(None, "lat", "lon", None),
        P(),
        P(),
        P(),
        P(),
        P(None, "lat", None, None),
        P(),
        P(None, "lat", "lon", None),
    )
    return jax.shard_map(
        on_device,
        mesh=mesh,
        in_specs=placed,
        out_specs=(
            P(None, "lat", "lon", None),
            P(None, "lat", "lon", None),
            P(),
            P(),
            P(),
            P(),
            P(None, "lat", None, None),
        ),
        check_vma=False,
    )
```

```python
import functools

import jax
import jax.numpy as jnp
from jax import lax
from jax.experimental import pallas as pl
from jax.experimental.pallas import tpu as pltpu
from jax.sharding import PartitionSpec as P

HEADS = 6
WZ = 2
WH = 6
WW = 12
BLOCK = WZ * WH
WIN = BLOCK * WW
SPANS = 2 * WW - 1
SPREAD = 384
LANES = 128
PAD_LEVEL = 8
SUBLANES = 8
TAIL = SPANS * BLOCK - 2 * LANES
TABLE_ROWS = 2 * HEADS * BLOCK + 16
LARGE = 1e30

epsilon = 1e-05

f32, bf16 = jnp.float32, jnp.bfloat16


def call(body, outs, scratch=(), flops=0, moved=0, **kwargs):
    return pl.pallas_call(
        body,
        out_shape=outs,
        scratch_shapes=list(scratch),
        compiler_params=pltpu.CompilerParams(vmem_limit_bytes=48 * 1024 * 1024),
        cost_estimate=pl.CostEstimate(flops=flops, bytes_accessed=moved, transcendentals=0),
        **kwargs,
    )


def struct(shape, dtype):
    return jax.ShapeDtypeStruct(shape, dtype)


def quotient(value, divisor):
    return (value * (65536 // divisor + 1)) >> 16


def columns(shape, dim):
    return lax.broadcasted_iota(jnp.int32, shape, dim)


def hot(condition):
    return jnp.where(condition, 1.0, 0.0).astype(bf16)


def quadrants(lat_rows, lon_cols):
    lat_cut, lon_cut = WH // 2, WW // 2
    high_lat, low_lat = slice(lat_cut, lat_rows), slice(lat_cut)
    high_lon, low_lon = slice(lon_cut, lon_cols), slice(lon_cut)
    return (high_lat, high_lon), (high_lat, low_lon), (low_lat, high_lon), (low_lat, low_lon)


def window_matrix(levels, room):
    lat_cut, lon_cut, level_cut = WH // 2, WW // 2, WZ // 2
    count = levels // WZ * WIN
    token = columns((count, 1), 0)
    window = quotient(token, WIN)
    inside = token - window * WIN
    lon = quotient(inside, BLOCK)
    cell = inside - lon * BLOCK
    depth = quotient(cell, WH)
    lat = cell - depth * WH
    level = window * WZ + depth + level_cut
    level = jnp.where(level >= levels, level - levels, level)
    late_lon, late_lat = lon >= lon_cut, lat >= lat_cut
    quad = jnp.where(late_lat, 2, 0) + jnp.where(late_lon, 1, 0)
    row = jnp.where(late_lat, lat - lat_cut, lat)
    col = jnp.where(late_lon, lon - lon_cut, lon)
    source = ((quad * lat_cut + row) * lon_cut + col) * room + level
    return hot(columns((count, WIN // WZ * room), 1) == source)


def pack_body(count, *refs):
    features, cotangent, *plain = refs[: count + 2]
    *outs, sems = refs[count + 2 :]
    lat_rows, lon_cols, _, _ = features.shape
    pairs = []
    for (rows, cols), out in zip(quadrants(lat_rows, lon_cols), outs):
        pairs += [(features.at[rows, cols], out.at[0]), (cotangent.at[rows, cols], out.at[1])]
    pairs += zip(plain, outs[4:])
    copies = [pltpu.make_async_copy(*pair, sems.at[at]) for at, pair in enumerate(pairs)]
    for copy in copies:
        copy.start()
    for copy in copies:
        copy.wait()


def unpack_body(here, from_lon, from_lat, from_both, outputs, grad_features):
    lat_rows, lon_cols, levels, width = outputs.shape
    for (rows, cols), quad in zip(
        quadrants(lat_rows, lon_cols), (here, from_lon, from_lat, from_both)
    ):
        tiles = quad[...].astype(f32).reshape(3, -1, LANES)
        rest = width - LANES
        pair = (
            jnp.concatenate((tiles[0], tiles[2][:, :rest]), 1),
            jnp.concatenate((tiles[1], tiles[2][:, rest:]), 1),
        )
        for value, out in zip(pair, (outputs, grad_features)):
            value = value.reshape(WH // 2, WW // 2, levels, width)
            out[rows, cols] = value.astype(bf16)


def spread_index(index_table):
    parts = []
    rows = [
        jnp.concatenate([index_table[c * WW + a : c * WW + a + 1, :] for c in range(BLOCK)], 0)
        for a in (WW - 1, 0)
    ]
    fill = jnp.zeros((16 - BLOCK, WIN), f32)
    token = columns((WIN, 1), 0)
    cell = quotient(token, WW)
    entry = (token - cell * WW) * BLOCK + cell
    wide = columns((WIN, SPREAD), 1)
    cut_at = (WW - 1) * BLOCK
    picks = (
        hot(jnp.logical_and(entry == wide, wide < cut_at)),
        hot(entry + cut_at == wide),
    )
    for cut in (lambda v: v >> 7, lambda v: v & (LANES - 1)):
        total = jnp.zeros((16, SPREAD), f32)
        for labels, pick in zip(rows, picks):
            value = jnp.concatenate((cut(labels).astype(f32), fill), 0).astype(bf16)
            total += jnp.dot(value, pick, preferred_element_type=f32)
        parts.append(total.astype(jnp.int32))
    return parts


def bias_body(bias_table, index_table, out, chunk_out, lane_out, table):
    level_win, heads, _, labels = bias_table.shape
    chunk, lane = spread_index(index_table)
    chunk_out[...] = chunk
    lane_out[...] = lane
    chunks = -(-labels // LANES)
    for t in range(level_win):
        for h in range(heads):
            table[t * heads + h : t * heads + h + 1, :labels] = bias_table[t, h]
    cell = columns((16, 1), 0)
    other = columns((1, SPREAD), 1)
    other = other - quotient(other, BLOCK) * BLOCK
    level_apart = (cell >= WH) != (other >= WH)
    cell = jnp.where(cell >= WH, cell - WH, cell)
    other = jnp.where(other >= WH, other - WH, other)
    row_apart = (cell >= WH // 2) != (other >= WH // 2)
    top = lax.axis_index("lat") == lax.axis_size("lat") - 1
    barred_rows = jnp.logical_and(row_apart, top)
    for t in range(level_win):
        barred = barred_rows
        if t == level_win - 1:
            barred = jnp.logical_or(barred, level_apart)
        for h in range(heads):
            row = t * heads + h
            tiles = []
            for tile in range(SPREAD // LANES):
                at = slice(tile * LANES, (tile + 1) * LANES)
                found = jnp.zeros((16, LANES), f32)
                for c in range(chunks):
                    source = jnp.broadcast_to(
                        table[row : row + 1, c * LANES : (c + 1) * LANES], (16, LANES)
                    )
                    taken = jnp.take_along_axis(source, lane[:, at], axis=1, mode="promise_in_bounds")
                    found = jnp.where(chunk[:, at] == c, taken, found)
                tiles.append(found)
            value = jnp.where(barred, -LARGE, jnp.concatenate(tiles, 1))
            for a in range(WW):
                shift = (WW - 1 - a) * BLOCK
                out[row, a * BLOCK : (a + 1) * BLOCK, :] = value[:BLOCK, shift : shift + WIN]


def inverse_body(chunk, lane, chunk_out, lane_out):
    pieces = SPREAD // LANES
    labels = chunk_out.shape[0]
    valid = SPANS * BLOCK
    total = jnp.zeros((2 * labels, LANES), f32)
    wide = lax.broadcasted_iota(jnp.int32, (labels, SPREAD), 1)
    tall = lax.broadcasted_iota(jnp.int32, (labels, SPREAD), 0)
    lanes = lax.broadcasted_iota(jnp.int32, (LANES, SPREAD), 0)
    for cell in range(BLOCK):
        own = jnp.logical_and(chunk[cell : cell + 1, :] == tall, wide < valid)
        piece = jnp.where(own, (cell * pieces + wide // LANES).astype(f32), 0.0)
        spot = jnp.where(own, (wide % LANES).astype(f32), 0.0)
        both = jnp.concatenate((piece, spot), 0).astype(bf16)
        hit = jnp.where(lane[cell : cell + 1, :] == lanes, 1.0, 0.0).astype(bf16)
        total += lax.dot_general(both, hit, (((1,), (1,)), ((), ())), preferred_element_type=f32)
    chunk_out[...] = total[:labels].astype(jnp.int32)
    lane_out[...] = total[labels:].astype(jnp.int32)


def place_body(blocks, piece, spot, out):
    pieces = SPREAD // LANES
    head = columns((SUBLANES, 1), 0)
    at_piece, at_spot, at_tail = [], [], []
    for c in range(out.shape[1] // LANES):
        at_piece.append(jnp.broadcast_to(piece[c : c + 1, :], (SUBLANES, LANES)))
        at_spot.append(jnp.broadcast_to(spot[c : c + 1, :], (SUBLANES, LANES)))
        at_tail.append((at_spot[c] + TAIL * head) & (LANES - 1))
    found = [jnp.zeros((SUBLANES, LANES), f32) for _ in at_piece]
    values = blocks[...].astype(f32).reshape(TABLE_ROWS, LANES)
    fill = jnp.zeros((SUBLANES - HEADS, LANES), f32)
    for cell in range(BLOCK):
        for tile in range(pieces):
            if tile < pieces - 1:
                starts = [(tile * HEADS + h) * BLOCK + cell for h in range(HEADS)]
                source = jnp.concatenate([values[r : r + 1] for r in starts] + [fill], 0)
                spots = at_spot
            else:
                row = tile * HEADS * BLOCK + cell
                source = jnp.broadcast_to(values[row : row + 1], (SUBLANES, LANES))
                spots = at_tail
            for c in range(len(found)):
                taken = jnp.take_along_axis(source, spots[c], axis=1, mode="promise_in_bounds")
                found[c] = jnp.where(at_piece[c] == cell * pieces + tile, taken, found[c])
    for c in range(len(found)):
        out[:, c * LANES : (c + 1) * LANES] = found[c].astype(bf16)


def window_body(
    here, from_lon, from_lat, from_both, norm_gain, norm_shift, w_qkv, w_out, bias,
    out_here, out_lon, out_lat, out_both, keep, send, gathered, proj_grad, sums, tables,
):
    width = w_out.shape[0]
    level_win = bias.shape[0] // HEADS
    head_size = width // HEADS
    scaling = head_size ** (-0.5)
    _, lat_half, lon_half, levels, _ = here.shape
    quad_rows = lat_half * lon_half * PAD_LEVEL
    fill = jnp.zeros((lat_half, lon_half, PAD_LEVEL - levels, width), f32)
    picks = window_matrix(levels, PAD_LEVEL)
    features, cotangent = (
        jnp.dot(
            picks,
            jnp.concatenate(
                [
                    jnp.concatenate((quad[at].astype(f32), fill), 2).reshape(quad_rows, width)
                    for quad in (here, from_lon, from_lat, from_both)
                ],
                0,
            ).astype(bf16),
            preferred_element_type=f32,
        )
        for at in range(2)
    )
    grad_shifted = cotangent.astype(bf16)
    gain = norm_gain[...]
    center = features - jnp.mean(features, -1, keepdims=True)
    inv_std = lax.rsqrt(jnp.mean(center * center, -1, keepdims=True) + epsilon)
    x_hat = center * inv_std
    normed = (x_hat * gain + norm_shift[...]).astype(bf16)
    query, key, value = (
        jnp.dot(normed, w_qkv[:, k * width : (k + 1) * width], preferred_element_type=f32).astype(bf16)
        for k in range(3)
    )
    grad_heads = lax.dot_general(
        grad_shifted, w_out[...], (((1,), (1,)), ((), ())), preferred_element_type=f32
    ).astype(bf16)
    head_of = lax.broadcasted_iota(jnp.int32, (1, width), 1) // head_size
    mixed_parts = []
    for t in range(level_win):
        rows = slice(t * WIN, (t + 1) * WIN)
        q, k, v, g = query[rows], key[rows], value[rows], grad_heads[rows]
        q_heads = [jnp.where(head_of == h, q, jnp.zeros_like(q)) for h in range(HEADS)]
        g_heads = [jnp.where(head_of == h, g, jnp.zeros_like(g)) for h in range(HEADS)]
        mixed = jnp.zeros((WIN, width), f32)
        grad_query = jnp.zeros((WIN, width), f32)
        grad_key = jnp.zeros((WIN, width), f32)
        grad_value = jnp.zeros((WIN, width), f32)
        for h in range(HEADS):
            logits = lax.dot_general(
                q_heads[h], k, (((1,), (1,)), ((), ())), preferred_element_type=f32
            )
            logits = logits * scaling + bias[t * HEADS + h]
            raised = jnp.exp(logits - jnp.max(logits, -1, keepdims=True))
            weights = raised * (1.0 / jnp.sum(raised, -1, keepdims=True))
            weights_bf = weights.astype(bf16)
            mixed = jnp.where(
                head_of == h, jnp.dot(weights_bf, v, preferred_element_type=f32), mixed
            )
            grad_weights = lax.dot_general(
                g_heads[h], v, (((1,), (1,)), ((), ())), preferred_element_type=f32
            )
            grad_value += lax.dot_general(
                weights_bf, g_heads[h], (((0,), (0,)), ((), ())), preferred_element_type=f32
            )
            grad_logits = weights * (
                grad_weights - jnp.sum(weights * grad_weights, -1, keepdims=True)
            )
            logit_bf = grad_logits.astype(bf16)
            grad_query = jnp.where(
                head_of == h, jnp.dot(logit_bf, k, preferred_element_type=f32), grad_query
            )
            grad_key += lax.dot_general(
                logit_bf, q_heads[h], (((0,), (0,)), ((), ())), preferred_element_type=f32
            )
            total = jnp.zeros((BLOCK, SPREAD), f32)
            for a in range(WW):
                shift = (WW - 1 - a) * BLOCK
                piece = grad_logits[a * BLOCK : (a + 1) * BLOCK]
                piece = jnp.concatenate((piece, jnp.zeros((BLOCK, SPREAD - WIN), f32)), 1)
                total += pltpu.roll(piece, shift, 1) if shift else piece
            for tile in range(2):
                row = (tile * HEADS + h) * BLOCK
                tables[t, row : row + BLOCK, :] = total[:, tile * LANES : (tile + 1) * LANES]
            last = total[:, 2 * LANES :]
            tails = tails + pltpu.roll(last, h * TAIL, 1) if h else last
        row = 2 * HEADS * BLOCK
        tables[t, row : row + BLOCK, :] = tails
        tables[t, row + BLOCK :, :] = jnp.zeros((TABLE_ROWS - row - BLOCK, LANES), f32)
        mixed_parts.append(mixed.astype(bf16))
        proj_grad[rows, :width] = (grad_query * scaling).astype(bf16)
        proj_grad[rows, width : 2 * width] = (grad_key * scaling).astype(bf16)
        proj_grad[rows, 2 * width :] = grad_value.astype(bf16)
    mixed = jnp.concatenate(mixed_parts, 0)
    attn = jnp.dot(mixed, w_out[...], preferred_element_type=f32).astype(bf16)
    outputs = (features + attn.astype(f32)).astype(bf16)
    grad_proj = proj_grad[...]
    grad_input = lax.dot_general(
        grad_proj, w_qkv[...], (((1,), (1,)), ((), ())), preferred_element_type=f32
    )
    upstream = grad_input.astype(bf16).astype(f32)
    gain_part = jnp.sum(upstream * x_hat, 0, keepdims=True)
    shift_part = jnp.sum(upstream, 0, keepdims=True)
    g_hat = upstream * gain
    centred = (
        g_hat
        - jnp.mean(g_hat, -1, keepdims=True)
        - x_hat * jnp.mean(g_hat * x_hat, -1, keepdims=True)
    )
    grad_features = (cotangent + inv_std * centred).astype(bf16)
    picks = window_matrix(levels, levels)
    back = [
        lax.dot_general(picks, result, (((0,), (0,)), ((), ())), preferred_element_type=f32)
        for result in (outputs, grad_features)
    ]
    rest = width - LANES
    tiles = [b[:, :LANES] for b in back]
    tiles.append(jnp.concatenate([b[:, LANES:] for b in back], 1))
    groups = lat_half * lon_half * levels // SUBLANES
    for at, tile in enumerate(tiles):
        tile = tile.astype(bf16).reshape(4, groups, SUBLANES, LANES)
        for q, out in enumerate((out_here, out_lon, out_lat, out_both)):
            out[at * groups : (at + 1) * groups] = tile[q]
    sums[:, : 3 * width] = lax.dot_general(
        normed, grad_proj, (((0,), (0,)), ((), ())), preferred_element_type=f32
    )
    sums[:, 3 * width :] = lax.dot_general(
        mixed, grad_shifted, (((0,), (0,)), ((), ())), preferred_element_type=f32
    )
    chunks, blocks, _, _ = gathered.shape
    lat_count = chunks // 2
    size = width // chunks
    fill = jnp.zeros((1, 2 * LANES - width), f32)
    ends = [gain_part[:, :LANES], jnp.concatenate((gain_part[:, LANES:], fill), 1)]
    ends += [shift_part[:, :LANES], jnp.concatenate((shift_part[:, LANES:], fill), 1)]
    ends = jnp.concatenate(ends + [jnp.zeros((SUBLANES - 4, LANES), f32)], 0).astype(bf16)
    for j in range(chunks):
        piece = jnp.concatenate(
            [
                sums[j * size : (j + 1) * size, b * LANES : (b + 1) * LANES]
                for b in range(4 * width // LANES)
            ],
            0,
        )
        gathered[j, : blocks - 1] = piece.reshape(blocks - 1, SUBLANES, LANES).astype(bf16)
        gathered[j, blocks - 1] = ends
    core = lax.axis_index("lon") % 2
    lat = lax.axis_index("lat")
    for half, out in enumerate((keep, send)):
        side = core ^ half
        for at in range(lat_count):
            out[at * blocks : (at + 1) * blocks] = gathered[
                side * lat_count + (lat ^ at)
            ]
        table = tables[side].reshape(TABLE_ROWS // SUBLANES, SUBLANES, LANES)
        out[lat_count * blocks :] = table.astype(bf16)


def tree(values):
    while len(values) > 1:
        values = [a + b for a, b in zip(values[::2], values[1::2])]
    return values[0]


def halves_body(keep, came, *outs):
    at = 0
    for out in outs:
        part = slice(at, at + out.shape[0])
        out[...] = (keep[part].astype(f32) + came[part].astype(f32)).astype(bf16)
        at += out.shape[0]


def lats_body(*refs):
    *pieces, tail, out = refs
    blocks = pieces[0].shape[0]
    out[:blocks] = tree([p[...].astype(f32) for p in pieces]).astype(bf16)
    out[blocks:] = tail[...]


def lons_body(count, *refs):
    pieces, (weights, tail) = refs[:count], refs[count:]
    blocks = weights.shape[0]
    total = tree([p[...].astype(f32) for p in pieces]).astype(bf16)
    weights[...] = total[:blocks]
    tail[...] = total[blocks:]


def finish_body(lat_count, factor, *refs):
    near, far = refs[:lat_count], refs[lat_count : 2 * lat_count]
    table_near, table_far, grad_gain, grad_shift, grad_wqkv, grad_wout, grad_table, chunks, halves = refs[
        2 * lat_count :
    ]
    core = lax.axis_index("lon") % 2
    lat = lax.axis_index("lat")
    count, blocks, _, _ = chunks.shape
    for half, group in enumerate((near, far)):
        for at, ref in enumerate(group):
            chunks[(core ^ half) * lat_count + (lat ^ at)] = ref[...].astype(f32) * factor
    halves[core] = table_near[...].astype(f32) * factor
    halves[core ^ 1] = table_far[...].astype(f32) * factor
    width = grad_wout.shape[0]
    size = width // count
    for j in range(count):
        rows = slice(j * size, (j + 1) * size)
        tall = chunks[j, : blocks - 1].reshape((blocks - 1) * SUBLANES, LANES)
        whole = jnp.concatenate(
            [tall[b * size : (b + 1) * size] for b in range(tall.shape[0] // size)], 1
        )
        grad_wqkv[rows, :] = whole[:, : 3 * width]
        grad_wout[rows, :] = whole[:, 3 * width :]
    rest = width - LANES
    for at, out in enumerate((grad_gain, grad_shift)):
        out[:, :LANES] = chunks[0, blocks - 1, 2 * at : 2 * at + 1]
        out[:, LANES:] = chunks[0, blocks - 1, 2 * at + 1 : 2 * at + 2, :rest]
    level_win, heads, _, labels = grad_table.shape
    for t in range(level_win):
        for h in range(heads):
            grad_table[t, h] = halves[t, h : h + 1, :labels]


def swap(value, axis, distance):
    count = lax.axis_size(axis)
    return lax.ppermute(value, axis, [(source, source ^ distance) for source in range(count)])


def shifted(value, lat_step, lon_step):
    lat_count, lon_count = lax.axis_size("lat"), lax.axis_size("lon")
    pairs = [
        (r * lon_count + c, (r + lat_step) % lat_count * lon_count + (c + lon_step) % lon_count)
        for r in range(lat_count)
        for c in range(lon_count)
    ]
    return lax.ppermute(value, ("lat", "lon"), pairs)


def on_device(features, norm_gain, norm_shift, w_qkv, w_out, bias_table, index_table, cotangent):
    levels, lat_rows, lon_cols, width = features.shape
    level_win, _, heads, labels = bias_table.shape
    lat_count, lon_count = lax.axis_size("lat"), lax.axis_size("lon")
    quad = struct((2, WH // 2, WW // 2, levels, width), bf16)
    steps = ((0, 1), (1, 0), (1, 1))

    plain = (
        norm_gain[None], norm_shift[None], w_qkv, w_out, bias_table.transpose(0, 2, 1, 3), index_table
    )
    far_side = pl.BlockSpec(memory_space=pltpu.HBM)
    *packed, gain, shift, w_qkv, w_out, table, labels_of = call(
        functools.partial(pack_body, len(plain)),
        (quad,) * 4 + tuple(struct(p.shape, p.dtype) for p in plain),
        [pltpu.SemaphoreType.DMA((8 + len(plain),))],
        in_specs=[far_side] * (2 + len(plain)),
    )(
        *(
            pltpu.with_memory_space_constraint(v, pltpu.HBM)
            for v in (features.transpose(1, 2, 0, 3), cotangent.transpose(1, 2, 0, 3), *plain)
        )
    )
    here, *edges = packed
    came = [shifted(e, -lat, -lon) for e, (lat, lon) in zip(edges, steps)]

    spread = struct((16, SPREAD), jnp.int32)
    whole_lanes = -(-labels // LANES) * LANES
    bias, chunk, lane = call(
        bias_body,
        (struct((level_win * heads, WIN, WIN), f32), spread, spread),
        [pltpu.VMEM((level_win * heads, whole_lanes), f32)],
        moved=16 * 10**6,
    )(table, labels_of)

    blocks = 4 * width * width // (2 * lat_count) // (SUBLANES * LANES) + 1
    table_blocks = TABLE_ROWS // SUBLANES
    quad_blocks = 2 * WH // 2 * WW // 2 * levels * width // (SUBLANES * LANES)

    def stack(count):
        return struct((count, SUBLANES, LANES), bf16)

    half = stack(lat_count * blocks + table_blocks)
    out_here, *backs, keep, send = call(
        window_body,
        (stack(quad_blocks),) * 4 + (half, half),
        [
            pltpu.VMEM((2 * lat_count, blocks, SUBLANES, LANES), bf16),
            pltpu.VMEM((level_win * WIN, 3 * width), bf16),
            pltpu.VMEM((width, 4 * width), f32),
            pltpu.VMEM((level_win, TABLE_ROWS, LANES), f32),
        ],
        moved=25 * 10**6,
    )(here, *came, gain, shift, w_qkv, w_out, bias)

    send, chunk, lane = lax.optimization_barrier((send, chunk, lane))
    came = swap(send, "lon", 1)
    places = struct((32, LANES), jnp.int32)
    piece, spot = call(inverse_body, (places, places), moved=2 * 10**6)(chunk, lane)
    came, piece, spot = lax.optimization_barrier((came, piece, spot))
    *pieces, tail = call(halves_body, (stack(blocks),) * lat_count + (stack(table_blocks),))(keep, came)
    pieces = [swap(p, "lat", at) if at else p for at, p in enumerate(pieces)]
    part = call(lats_body, stack(blocks + table_blocks))(*pieces, tail)
    parts = [part] + [swap(part, "lon", 2 * at) for at in range(1, lon_count // 2)]
    returned = [shifted(b, lat, lon) for b, (lat, lon) in zip(backs, steps)]
    weights, tail = call(functools.partial(lons_body, len(parts)), (stack(blocks), stack(table_blocks)))(
        *parts
    )
    near = [weights] + [swap(weights, "lat", at) for at in range(1, lat_count)]
    table_near = call(place_body, struct((SUBLANES, whole_lanes), bf16), moved=5 * 10**6)(
        tail, piece, spot
    )
    table_far = swap(table_near, "lon", 1)
    far = [swap(n, "lon", 1) for n in near]

    cells = struct((lat_rows, lon_cols, levels, width), bf16)
    outputs, grad_features = call(unpack_body, (cells, cells), moved=2 * 10**6)(
        out_here, *returned
    )
    factor = (levels * lat_rows * lat_count * lon_cols * lon_count) ** (-0.5)
    row = struct((1, width), f32)
    grad_gain, grad_shift, grad_wqkv, grad_wout, grad_table = call(
        functools.partial(finish_body, lat_count, factor),
        (
            row,
            row,
            struct(w_qkv.shape, f32),
            struct(w_out.shape, f32),
            struct((level_win, heads, 1, labels), f32),
        ),
        [
            pltpu.VMEM((2 * lat_count, blocks, SUBLANES, LANES), f32),
            pltpu.VMEM((2,) + table_near.shape, f32),
        ],
    )(*near, *far, table_near, table_far)
    return (
        outputs.transpose(2, 0, 1, 3),
        grad_features.transpose(2, 0, 1, 3),
        grad_gain[0],
        grad_shift[0],
        grad_wqkv,
        grad_wout,
        grad_table.transpose(0, 2, 1, 3),
    )


def solution(mesh):
    placed = (
        P(None, "lat", "lon", None),
        P(),
        P(),
        P(),
        P(),
        P(None, "lat", None, None),
        P(),
        P(None, "lat", "lon", None),
    )
    return jax.shard_map(
        on_device,
        mesh=mesh,
        in_specs=placed,
        out_specs=(
            P(None, "lat", "lon", None),
            P(None, "lat", "lon", None),
            P(),
            P(),
            P(),
            P(),
            P(None, "lat", None, None),
        ),
        check_vma=False,
    )
```

```python
import functools

import jax
import jax.numpy as jnp
from jax import lax
from jax.experimental import pallas as pl
from jax.experimental.pallas import tpu as pltpu
from jax.sharding import PartitionSpec as P

HEADS = 6
WZ = 2
WH = 6
WW = 12
BLOCK = WZ * WH
WIN = BLOCK * WW
SPANS = 2 * WW - 1
SPREAD = 384
LANES = 128
PAD_LEVEL = 8
SUBLANES = 8
TAIL = SPANS * BLOCK - 2 * LANES
TABLE_ROWS = 2 * HEADS * BLOCK + 16
LARGE = 1e30

epsilon = 1e-05

f32, bf16 = jnp.float32, jnp.bfloat16


def call(body, outs, scratch=(), flops=0, moved=0, **kwargs):
    return pl.pallas_call(
        body,
        out_shape=outs,
        scratch_shapes=list(scratch),
        compiler_params=pltpu.CompilerParams(vmem_limit_bytes=48 * 1024 * 1024),
        cost_estimate=pl.CostEstimate(flops=flops, bytes_accessed=moved, transcendentals=0),
        **kwargs,
    )


def struct(shape, dtype):
    return jax.ShapeDtypeStruct(shape, dtype)


def quotient(value, divisor):
    return (value * (65536 // divisor + 1)) >> 16


def columns(shape, dim):
    return lax.broadcasted_iota(jnp.int32, shape, dim)


def hot(condition):
    return jnp.where(condition, 1.0, 0.0).astype(bf16)


def quadrants(lat_rows, lon_cols):
    lat_cut, lon_cut = WH // 2, WW // 2
    high_lat, low_lat = slice(lat_cut, lat_rows), slice(lat_cut)
    high_lon, low_lon = slice(lon_cut, lon_cols), slice(lon_cut)
    return (high_lat, high_lon), (high_lat, low_lon), (low_lat, high_lon), (low_lat, low_lon)


def window_matrix(levels, room):
    lat_cut, lon_cut, level_cut = WH // 2, WW // 2, WZ // 2
    count = levels // WZ * WIN
    token = columns((count, 1), 0)
    window = quotient(token, WIN)
    inside = token - window * WIN
    lon = quotient(inside, BLOCK)
    cell = inside - lon * BLOCK
    depth = quotient(cell, WH)
    lat = cell - depth * WH
    level = window * WZ + depth + level_cut
    level = jnp.where(level >= levels, level - levels, level)
    late_lon, late_lat = lon >= lon_cut, lat >= lat_cut
    quad = jnp.where(late_lat, 2, 0) + jnp.where(late_lon, 1, 0)
    row = jnp.where(late_lat, lat - lat_cut, lat)
    col = jnp.where(late_lon, lon - lon_cut, lon)
    source = ((quad * lat_cut + row) * lon_cut + col) * room + level
    return hot(columns((count, WIN // WZ * room), 1) == source)


def pack_body(count, *refs):
    features, cotangent, *plain = refs[: count + 2]
    *outs, sems = refs[count + 2 :]
    lat_rows, lon_cols, _, _ = features.shape
    pairs = []
    for (rows, cols), out in zip(quadrants(lat_rows, lon_cols), outs):
        pairs += [(features.at[rows, cols], out.at[0]), (cotangent.at[rows, cols], out.at[1])]
    pairs += zip(plain, outs[4:])
    copies = [pltpu.make_async_copy(*pair, sems.at[at]) for at, pair in enumerate(pairs)]
    for copy in copies:
        copy.start()
    for copy in copies:
        copy.wait()


def unpack_body(here, from_lon, from_lat, from_both, outputs, grad_features):
    lat_rows, lon_cols, levels, width = outputs.shape
    for (rows, cols), quad in zip(
        quadrants(lat_rows, lon_cols), (here, from_lon, from_lat, from_both)
    ):
        tiles = quad[...].astype(f32).reshape(3, -1, LANES)
        rest = width - LANES
        pair = (
            jnp.concatenate((tiles[0], tiles[2][:, :rest]), 1),
            jnp.concatenate((tiles[1], tiles[2][:, rest:]), 1),
        )
        for value, out in zip(pair, (outputs, grad_features)):
            value = value.reshape(WH // 2, WW // 2, levels, width)
            out[rows, cols] = value.astype(bf16)


def spread_index(index_table):
    parts = []
    rows = [
        jnp.concatenate([index_table[c * WW + a : c * WW + a + 1, :] for c in range(BLOCK)], 0)
        for a in (WW - 1, 0)
    ]
    fill = jnp.zeros((16 - BLOCK, WIN), f32)
    token = columns((WIN, 1), 0)
    cell = quotient(token, WW)
    entry = (token - cell * WW) * BLOCK + cell
    wide = columns((WIN, SPREAD), 1)
    cut_at = (WW - 1) * BLOCK
    picks = (
        hot(jnp.logical_and(entry == wide, wide < cut_at)),
        hot(entry + cut_at == wide),
    )
    for cut in (lambda v: v >> 7, lambda v: v & (LANES - 1)):
        total = jnp.zeros((16, SPREAD), f32)
        for labels, pick in zip(rows, picks):
            value = jnp.concatenate((cut(labels).astype(f32), fill), 0).astype(bf16)
            total += jnp.dot(value, pick, preferred_element_type=f32)
        parts.append(total.astype(jnp.int32))
    return parts


def bias_body(bias_table, index_table, out, chunk_out, lane_out, table):
    level_win, heads, _, labels = bias_table.shape
    chunk, lane = spread_index(index_table)
    chunk_out[...] = chunk
    lane_out[...] = lane
    chunks = -(-labels // LANES)
    for t in range(level_win):
        for h in range(heads):
            table[t * heads + h : t * heads + h + 1, :labels] = bias_table[t, h]
    cell = columns((16, 1), 0)
    other = columns((1, SPREAD), 1)
    other = other - quotient(other, BLOCK) * BLOCK
    level_apart = (cell >= WH) != (other >= WH)
    cell = jnp.where(cell >= WH, cell - WH, cell)
    other = jnp.where(other >= WH, other - WH, other)
    row_apart = (cell >= WH // 2) != (other >= WH // 2)
    top = lax.axis_index("lat") == lax.axis_size("lat") - 1
    barred_rows = jnp.logical_and(row_apart, top)
    rest = BLOCK - SUBLANES
    sub = columns((SUBLANES, LANES), 0)
    early = sub < rest

    def spread_row(row):
        return jnp.broadcast_to(row, (SUBLANES, LANES))

    def take(source, index):
        return jnp.take_along_axis(source, index, axis=1, mode="promise_in_bounds")

    tiles = SPREAD // LANES - 1
    upper, lower = [], []
    for tile in range(tiles):
        at = slice(tile * LANES, (tile + 1) * LANES)
        upper.append((chunk[:SUBLANES, at], lane[:SUBLANES, at]))
        lower.append(
            tuple(
                jnp.concatenate((v[SUBLANES:BLOCK, at], v[SUBLANES:BLOCK, at]), 0)
                for v in (chunk, lane)
            )
        )
    per = BLOCK // 2
    tails = []
    for first in (0, per):
        packed = []
        for v in (chunk, lane):
            total = v[first : first + 1, tiles * LANES :]
            for i in range(1, per):
                row = v[first + i : first + i + 1, tiles * LANES :]
                total = total + pltpu.roll(row, i * TAIL, 1)
            packed.append(spread_row(total))
        tails.append(packed)
    mixed_tail = [jnp.where(early, x, y) for x, y in zip(*tails)]
    rows = level_win * heads
    tail_found = [jnp.zeros((SUBLANES, LANES), f32) for _ in range(3)]
    for c in range(chunks):
        at = slice(c * LANES, (c + 1) * LANES)
        first = table[:SUBLANES, at]
        second = jnp.concatenate((table[SUBLANES:rows, at], table[SUBLANES:rows, at]), 0)
        for k, (source, (which, spot)) in enumerate(
            ((first, tails[0]), (first, tails[1]), (second, mixed_tail))
        ):
            tail_found[k] = jnp.where(which == c, take(source, spot), tail_found[k])
    cell = columns((SUBLANES, LANES), 0)
    entry = columns((SUBLANES, LANES), 1)
    upper_spot = (jnp.where(cell >= per, cell - per, cell) * TAIL + entry) & (LANES - 1)
    lower_cell = jnp.where(early, cell, cell - rest) + SUBLANES - per
    lower_spot = (lower_cell * TAIL + entry) & (LANES - 1)

    for row in range(0, rows, 2):
        pair = (row, row + 1)
        found = [[jnp.zeros((SUBLANES, LANES), f32) for _ in range(3)] for _ in range(tiles)]
        for c in range(chunks):
            sources = [
                spread_row(table[r : r + 1, c * LANES : (c + 1) * LANES]) for r in pair
            ]
            sources.append(jnp.where(early, *sources))
            for tile in range(tiles):
                for k, (which, spot) in enumerate((upper[tile], upper[tile], lower[tile])):
                    found[tile][k] = jnp.where(which == c, take(sources[k], spot), found[tile][k])
        ends = []
        for r in pair:
            if r < SUBLANES:
                ends.append([spread_row(tail_found[k][r : r + 1]) for k in range(2)])
            else:
                at = r - SUBLANES
                ends.append([spread_row(tail_found[2][i : i + 1]) for i in (at, rest + at)])
        last = [take(jnp.where(sub < per, *end), upper_spot) for end in ends]
        last.append(take(jnp.where(early, ends[0][1], ends[1][1]), lower_spot))
        found.append(last)
        for k, r in enumerate(pair):
            value = jnp.concatenate(
                [jnp.concatenate((f[k], f[2][k * rest : (k + 1) * rest]), 0) for f in found], 1
            )
            barred = barred_rows
            if r // heads == level_win - 1:
                barred = jnp.logical_or(barred, level_apart)
            value = jnp.where(barred[:BLOCK], -LARGE, value)
            for a in range(WW):
                shift = (WW - 1 - a) * BLOCK
                out[r, a * BLOCK : (a + 1) * BLOCK, :] = value[:, shift : shift + WIN]


def inverse_body(chunk, lane, chunk_out, lane_out):
    pieces = SPREAD // LANES
    labels = chunk_out.shape[0]
    valid = SPANS * BLOCK
    total = jnp.zeros((2 * labels, LANES), f32)
    wide = lax.broadcasted_iota(jnp.int32, (labels, SPREAD), 1)
    tall = lax.broadcasted_iota(jnp.int32, (labels, SPREAD), 0)
    lanes = lax.broadcasted_iota(jnp.int32, (LANES, SPREAD), 0)
    for cell in range(BLOCK):
        own = jnp.logical_and(chunk[cell : cell + 1, :] == tall, wide < valid)
        piece = jnp.where(own, (cell * pieces + wide // LANES).astype(f32), 0.0)
        spot = jnp.where(own, (wide % LANES).astype(f32), 0.0)
        both = jnp.concatenate((piece, spot), 0).astype(bf16)
        hit = jnp.where(lane[cell : cell + 1, :] == lanes, 1.0, 0.0).astype(bf16)
        total += lax.dot_general(both, hit, (((1,), (1,)), ((), ())), preferred_element_type=f32)
    chunk_out[...] = total[:labels].astype(jnp.int32)
    lane_out[...] = total[labels:].astype(jnp.int32)


def place_body(blocks, piece, spot, out):
    pieces = SPREAD // LANES
    head = columns((SUBLANES, 1), 0)
    at_piece, at_spot, at_tail = [], [], []
    for c in range(out.shape[1] // LANES):
        at_piece.append(jnp.broadcast_to(piece[c : c + 1, :], (SUBLANES, LANES)))
        at_spot.append(jnp.broadcast_to(spot[c : c + 1, :], (SUBLANES, LANES)))
        at_tail.append((at_spot[c] + TAIL * head) & (LANES - 1))
    found = [jnp.zeros((SUBLANES, LANES), f32) for _ in at_piece]
    values = blocks[...].astype(f32).reshape(TABLE_ROWS, LANES)
    fill = jnp.zeros((SUBLANES - HEADS, LANES), f32)
    for cell in range(BLOCK):
        for tile in range(pieces):
            if tile < pieces - 1:
                starts = [(tile * HEADS + h) * BLOCK + cell for h in range(HEADS)]
                source = jnp.concatenate([values[r : r + 1] for r in starts] + [fill], 0)
                spots = at_spot
            else:
                row = tile * HEADS * BLOCK + cell
                source = jnp.broadcast_to(values[row : row + 1], (SUBLANES, LANES))
                spots = at_tail
            for c in range(len(found)):
                taken = jnp.take_along_axis(source, spots[c], axis=1, mode="promise_in_bounds")
                found[c] = jnp.where(at_piece[c] == cell * pieces + tile, taken, found[c])
    for c in range(len(found)):
        out[:, c * LANES : (c + 1) * LANES] = found[c].astype(bf16)


def window_body(
    here, from_lon, from_lat, from_both, norm_gain, norm_shift, w_qkv, w_out, bias,
    out_here, out_lon, out_lat, out_both, keep, send, gathered, proj_grad, sums, tables,
):
    width = w_out.shape[0]
    level_win = bias.shape[0] // HEADS
    head_size = width // HEADS
    scaling = head_size ** (-0.5)
    _, lat_half, lon_half, levels, _ = here.shape
    quad_rows = lat_half * lon_half * PAD_LEVEL
    fill = jnp.zeros((lat_half, lon_half, PAD_LEVEL - levels, width), f32)
    picks = window_matrix(levels, PAD_LEVEL)
    features, cotangent = (
        jnp.dot(
            picks,
            jnp.concatenate(
                [
                    jnp.concatenate((quad[at].astype(f32), fill), 2).reshape(quad_rows, width)
                    for quad in (here, from_lon, from_lat, from_both)
                ],
                0,
            ).astype(bf16),
            preferred_element_type=f32,
        )
        for at in range(2)
    )
    grad_shifted = cotangent.astype(bf16)
    gain = norm_gain[...]
    center = features - jnp.mean(features, -1, keepdims=True)
    inv_std = lax.rsqrt(jnp.mean(center * center, -1, keepdims=True) + epsilon)
    x_hat = center * inv_std
    normed = (x_hat * gain + norm_shift[...]).astype(bf16)
    query, key, value = (
        jnp.dot(normed, w_qkv[:, k * width : (k + 1) * width], preferred_element_type=f32).astype(bf16)
        for k in range(3)
    )
    grad_heads = lax.dot_general(
        grad_shifted, w_out[...], (((1,), (1,)), ((), ())), preferred_element_type=f32
    ).astype(bf16)
    head_of = lax.broadcasted_iota(jnp.int32, (1, width), 1) // head_size
    mixed_parts = []
    for t in range(level_win):
        rows = slice(t * WIN, (t + 1) * WIN)
        q, k, v, g = query[rows], key[rows], value[rows], grad_heads[rows]
        q_heads = [jnp.where(head_of == h, q, jnp.zeros_like(q)) for h in range(HEADS)]
        g_heads = [jnp.where(head_of == h, g, jnp.zeros_like(g)) for h in range(HEADS)]
        q_heads = jnp.concatenate(q_heads, 0)
        g_heads = jnp.concatenate(g_heads, 0)
        all_logits = lax.dot_general(
            q_heads, k, (((1,), (1,)), ((), ())), preferred_element_type=f32
        )
        all_grads = lax.dot_general(
            g_heads, v, (((1,), (1,)), ((), ())), preferred_element_type=f32
        )
        mixed = jnp.zeros((WIN, width), f32)
        grad_query = jnp.zeros((WIN, width), f32)
        all_weights, all_logit_grads = [], []
        for h in range(HEADS):
            span = slice(h * WIN, (h + 1) * WIN)
            logits = all_logits[span] * scaling + bias[t * HEADS + h]
            raised = jnp.exp(logits - jnp.max(logits, -1, keepdims=True))
            weights = raised * (1.0 / jnp.sum(raised, -1, keepdims=True))
            weights_bf = weights.astype(bf16)
            mixed = jnp.where(
                head_of == h, jnp.dot(weights_bf, v, preferred_element_type=f32), mixed
            )
            grad_weights = all_grads[span]
            grad_logits = weights * (
                grad_weights - jnp.sum(weights * grad_weights, -1, keepdims=True)
            )
            logit_bf = grad_logits.astype(bf16)
            grad_query = jnp.where(
                head_of == h, jnp.dot(logit_bf, k, preferred_element_type=f32), grad_query
            )
            all_weights.append(weights_bf)
            all_logit_grads.append(logit_bf)
            total = jnp.zeros((BLOCK, SPREAD), f32)
            for a in range(WW):
                shift = (WW - 1 - a) * BLOCK
                piece = grad_logits[a * BLOCK : (a + 1) * BLOCK]
                piece = jnp.concatenate((piece, jnp.zeros((BLOCK, SPREAD - WIN), f32)), 1)
                total += pltpu.roll(piece, shift, 1) if shift else piece
            for tile in range(2):
                row = (tile * HEADS + h) * BLOCK
                tables[t, row : row + BLOCK, :] = total[:, tile * LANES : (tile + 1) * LANES]
            last = total[:, 2 * LANES :]
            tails = tails + pltpu.roll(last, h * TAIL, 1) if h else last
        row = 2 * HEADS * BLOCK
        tables[t, row : row + BLOCK, :] = tails
        tables[t, row + BLOCK :, :] = jnp.zeros((TABLE_ROWS - row - BLOCK, LANES), f32)
        grad_value, grad_key = (
            lax.dot_general(
                jnp.concatenate(left, 0), right, (((0,), (0,)), ((), ())), preferred_element_type=f32
            )
            for left, right in ((all_weights, g_heads), (all_logit_grads, q_heads))
        )
        mixed_parts.append(mixed.astype(bf16))
        proj_grad[rows, :width] = (grad_query * scaling).astype(bf16)
        proj_grad[rows, width : 2 * width] = (grad_key * scaling).astype(bf16)
        proj_grad[rows, 2 * width :] = grad_value.astype(bf16)
    mixed = jnp.concatenate(mixed_parts, 0)
    attn = jnp.dot(mixed, w_out[...], preferred_element_type=f32).astype(bf16)
    outputs = (features + attn.astype(f32)).astype(bf16)
    grad_proj = proj_grad[...]
    grad_input = lax.dot_general(
        grad_proj, w_qkv[...], (((1,), (1,)), ((), ())), preferred_element_type=f32
    )
    upstream = grad_input.astype(bf16).astype(f32)
    gain_part = jnp.sum(upstream * x_hat, 0, keepdims=True)
    shift_part = jnp.sum(upstream, 0, keepdims=True)
    g_hat = upstream * gain
    centred = (
        g_hat
        - jnp.mean(g_hat, -1, keepdims=True)
        - x_hat * jnp.mean(g_hat * x_hat, -1, keepdims=True)
    )
    grad_features = (cotangent + inv_std * centred).astype(bf16)
    picks = window_matrix(levels, levels)
    back = [
        lax.dot_general(picks, result, (((0,), (0,)), ((), ())), preferred_element_type=f32)
        for result in (outputs, grad_features)
    ]
    rest = width - LANES
    tiles = [b[:, :LANES] for b in back]
    tiles.append(jnp.concatenate([b[:, LANES:] for b in back], 1))
    groups = lat_half * lon_half * levels // SUBLANES
    for at, tile in enumerate(tiles):
        tile = tile.astype(bf16).reshape(4, groups, SUBLANES, LANES)
        for q, out in enumerate((out_here, out_lon, out_lat, out_both)):
            out[at * groups : (at + 1) * groups] = tile[q]
    sums[:, : 3 * width] = lax.dot_general(
        normed, grad_proj, (((0,), (0,)), ((), ())), preferred_element_type=f32
    )
    sums[:, 3 * width :] = lax.dot_general(
        mixed, grad_shifted, (((0,), (0,)), ((), ())), preferred_element_type=f32
    )
    chunks, blocks, _, _ = gathered.shape
    lat_count = chunks // 2
    size = width // chunks
    fill = jnp.zeros((1, 2 * LANES - width), f32)
    ends = [gain_part[:, :LANES], jnp.concatenate((gain_part[:, LANES:], fill), 1)]
    ends += [shift_part[:, :LANES], jnp.concatenate((shift_part[:, LANES:], fill), 1)]
    ends = jnp.concatenate(ends + [jnp.zeros((SUBLANES - 4, LANES), f32)], 0).astype(bf16)
    for j in range(chunks):
        piece = jnp.concatenate(
            [
                sums[j * size : (j + 1) * size, b * LANES : (b + 1) * LANES]
                for b in range(4 * width // LANES)
            ],
            0,
        )
        gathered[j, : blocks - 1] = piece.reshape(blocks - 1, SUBLANES, LANES).astype(bf16)
        gathered[j, blocks - 1] = ends
    core = lax.axis_index("lon") % 2
    lat = lax.axis_index("lat")
    for half, out in enumerate((keep, send)):
        side = core ^ half
        for at in range(lat_count):
            out[at * blocks : (at + 1) * blocks] = gathered[
                side * lat_count + (lat ^ at)
            ]
        table = tables[side].reshape(TABLE_ROWS // SUBLANES, SUBLANES, LANES)
        out[lat_count * blocks :] = table.astype(bf16)


def tree(values):
    while len(values) > 1:
        values = [a + b for a, b in zip(values[::2], values[1::2])]
    return values[0]


def halves_body(keep, came, *outs):
    at = 0
    for out in outs:
        part = slice(at, at + out.shape[0])
        out[...] = (keep[part].astype(f32) + came[part].astype(f32)).astype(bf16)
        at += out.shape[0]


def lats_body(*refs):
    *pieces, tail, out = refs
    blocks = pieces[0].shape[0]
    out[:blocks] = tree([p[...].astype(f32) for p in pieces]).astype(bf16)
    out[blocks:] = tail[...]


def lons_body(count, *refs):
    pieces, (weights, tail) = refs[:count], refs[count:]
    blocks = weights.shape[0]
    total = tree([p[...].astype(f32) for p in pieces]).astype(bf16)
    weights[...] = total[:blocks]
    tail[...] = total[blocks:]


def finish_body(lat_count, factor, *refs):
    near, far = refs[:lat_count], refs[lat_count : 2 * lat_count]
    table_near, table_far, grad_gain, grad_shift, grad_wqkv, grad_wout, grad_table, chunks, halves = refs[
        2 * lat_count :
    ]
    core = lax.axis_index("lon") % 2
    lat = lax.axis_index("lat")
    count, blocks, _, _ = chunks.shape
    for half, group in enumerate((near, far)):
        for at, ref in enumerate(group):
            chunks[(core ^ half) * lat_count + (lat ^ at)] = ref[...].astype(f32) * factor
    halves[core] = table_near[...].astype(f32) * factor
    halves[core ^ 1] = table_far[...].astype(f32) * factor
    width = grad_wout.shape[0]
    size = width // count
    for j in range(count):
        rows = slice(j * size, (j + 1) * size)
        tall = chunks[j, : blocks - 1].reshape((blocks - 1) * SUBLANES, LANES)
        whole = jnp.concatenate(
            [tall[b * size : (b + 1) * size] for b in range(tall.shape[0] // size)], 1
        )
        grad_wqkv[rows, :] = whole[:, : 3 * width]
        grad_wout[rows, :] = whole[:, 3 * width :]
    rest = width - LANES
    for at, out in enumerate((grad_gain, grad_shift)):
        out[:, :LANES] = chunks[0, blocks - 1, 2 * at : 2 * at + 1]
        out[:, LANES:] = chunks[0, blocks - 1, 2 * at + 1 : 2 * at + 2, :rest]
    level_win, heads, _, labels = grad_table.shape
    for t in range(level_win):
        for h in range(heads):
            grad_table[t, h] = halves[t, h : h + 1, :labels]


def swap(value, axis, distance):
    count = lax.axis_size(axis)
    return lax.ppermute(value, axis, [(source, source ^ distance) for source in range(count)])


def shifted(value, lat_step, lon_step):
    lat_count, lon_count = lax.axis_size("lat"), lax.axis_size("lon")
    pairs = [
        (r * lon_count + c, (r + lat_step) % lat_count * lon_count + (c + lon_step) % lon_count)
        for r in range(lat_count)
        for c in range(lon_count)
    ]
    return lax.ppermute(value, ("lat", "lon"), pairs)


def on_device(features, norm_gain, norm_shift, w_qkv, w_out, bias_table, index_table, cotangent):
    levels, lat_rows, lon_cols, width = features.shape
    level_win, _, heads, labels = bias_table.shape
    lat_count, lon_count = lax.axis_size("lat"), lax.axis_size("lon")
    quad = struct((2, WH // 2, WW // 2, levels, width), bf16)
    steps = ((0, 1), (1, 0), (1, 1))

    plain = (
        norm_gain[None], norm_shift[None], w_qkv, w_out, bias_table.transpose(0, 2, 1, 3), index_table
    )
    far_side = pl.BlockSpec(memory_space=pltpu.HBM)
    *packed, gain, shift, w_qkv, w_out, table, labels_of = call(
        functools.partial(pack_body, len(plain)),
        (quad,) * 4 + tuple(struct(p.shape, p.dtype) for p in plain),
        [pltpu.SemaphoreType.DMA((8 + len(plain),))],
        in_specs=[far_side] * (2 + len(plain)),
    )(
        *(
            pltpu.with_memory_space_constraint(v, pltpu.HBM)
            for v in (features.transpose(1, 2, 0, 3), cotangent.transpose(1, 2, 0, 3), *plain)
        )
    )
    here, *edges = packed
    came = [shifted(e, -lat, -lon) for e, (lat, lon) in zip(edges, steps)]

    spread = struct((16, SPREAD), jnp.int32)
    whole_lanes = -(-labels // LANES) * LANES
    bias, chunk, lane = call(
        bias_body,
        (struct((level_win * heads, WIN, WIN), f32), spread, spread),
        [pltpu.VMEM((level_win * heads, whole_lanes), f32)],
        moved=16 * 10**6,
    )(table, labels_of)

    blocks = 4 * width * width // (2 * lat_count) // (SUBLANES * LANES) + 1
    table_blocks = TABLE_ROWS // SUBLANES
    quad_blocks = 2 * WH // 2 * WW // 2 * levels * width // (SUBLANES * LANES)

    def stack(count):
        return struct((count, SUBLANES, LANES), bf16)

    half = stack(lat_count * blocks + table_blocks)
    out_here, *backs, keep, send = call(
        window_body,
        (stack(quad_blocks),) * 4 + (half, half),
        [
            pltpu.VMEM((2 * lat_count, blocks, SUBLANES, LANES), bf16),
            pltpu.VMEM((level_win * WIN, 3 * width), bf16),
            pltpu.VMEM((width, 4 * width), f32),
            pltpu.VMEM((level_win, TABLE_ROWS, LANES), f32),
        ],
        moved=25 * 10**6,
    )(here, *came, gain, shift, w_qkv, w_out, bias)

    send, chunk, lane = lax.optimization_barrier((send, chunk, lane))
    came = swap(send, "lon", 1)
    places = struct((32, LANES), jnp.int32)
    piece, spot = call(inverse_body, (places, places), moved=2 * 10**6)(chunk, lane)
    came, piece, spot = lax.optimization_barrier((came, piece, spot))
    *pieces, tail = call(halves_body, (stack(blocks),) * lat_count + (stack(table_blocks),))(keep, came)
    pieces = [swap(p, "lat", at) if at else p for at, p in enumerate(pieces)]
    part = call(lats_body, stack(blocks + table_blocks))(*pieces, tail)
    parts = [part] + [swap(part, "lon", 2 * at) for at in range(1, lon_count // 2)]
    returned = [shifted(b, lat, lon) for b, (lat, lon) in zip(backs, steps)]
    weights, tail = call(functools.partial(lons_body, len(parts)), (stack(blocks), stack(table_blocks)))(
        *parts
    )
    near = [weights] + [swap(weights, "lat", at) for at in range(1, lat_count)]
    table_near = call(place_body, struct((SUBLANES, whole_lanes), bf16), moved=5 * 10**6)(
        tail, piece, spot
    )
    table_far = swap(table_near, "lon", 1)
    far = [swap(n, "lon", 1) for n in near]

    cells = struct((lat_rows, lon_cols, levels, width), bf16)
    outputs, grad_features = call(unpack_body, (cells, cells), moved=2 * 10**6)(
        out_here, *returned
    )
    factor = (levels * lat_rows * lat_count * lon_cols * lon_count) ** (-0.5)
    row = struct((1, width), f32)
    grad_gain, grad_shift, grad_wqkv, grad_wout, grad_table = call(
        functools.partial(finish_body, lat_count, factor),
        (
            row,
            row,
            struct(w_qkv.shape, f32),
            struct(w_out.shape, f32),
            struct((level_win, heads, 1, labels), f32),
        ),
        [
            pltpu.VMEM((2 * lat_count, blocks, SUBLANES, LANES), f32),
            pltpu.VMEM((2,) + table_near.shape, f32),
        ],
    )(*near, *far, table_near, table_far)
    return (
        outputs.transpose(2, 0, 1, 3),
        grad_features.transpose(2, 0, 1, 3),
        grad_gain[0],
        grad_shift[0],
        grad_wqkv,
        grad_wout,
        grad_table.transpose(0, 2, 1, 3),
    )


def solution(mesh):
    placed = (
        P(None, "lat", "lon", None),
        P(),
        P(),
        P(),
        P(),
        P(None, "lat", None, None),
        P(),
        P(None, "lat", "lon", None),
    )
    return jax.shard_map(
        on_device,
        mesh=mesh,
        in_specs=placed,
        out_specs=(
            P(None, "lat", "lon", None),
            P(None, "lat", "lon", None),
            P(),
            P(),
            P(),
            P(),
            P(None, "lat", None, None),
        ),
        check_vma=False,
    )
```

```python
import functools

import jax
import jax.numpy as jnp
from jax import lax
from jax.experimental import pallas as pl
from jax.experimental.pallas import tpu as pltpu
from jax.sharding import PartitionSpec as P

HEADS = 6
WZ = 2
WH = 6
WW = 12
BLOCK = WZ * WH
WIN = BLOCK * WW
SPANS = 2 * WW - 1
SPREAD = 384
LANES = 128
PAD_LEVEL = 8
SUBLANES = 8
TAIL = SPANS * BLOCK - 2 * LANES
TABLE_ROWS = 2 * HEADS * BLOCK + 16
LARGE = 1e30

epsilon = 1e-05

f32, bf16 = jnp.float32, jnp.bfloat16


def call(body, outs, scratch=(), flops=0, moved=0, **kwargs):
    return pl.pallas_call(
        body,
        out_shape=outs,
        scratch_shapes=list(scratch),
        compiler_params=pltpu.CompilerParams(vmem_limit_bytes=48 * 1024 * 1024),
        cost_estimate=pl.CostEstimate(flops=flops, bytes_accessed=moved, transcendentals=0),
        **kwargs,
    )


def struct(shape, dtype):
    return jax.ShapeDtypeStruct(shape, dtype)


def quotient(value, divisor):
    return (value * (65536 // divisor + 1)) >> 16


def columns(shape, dim):
    return lax.broadcasted_iota(jnp.int32, shape, dim)


def hot(condition):
    return jnp.where(condition, 1.0, 0.0).astype(bf16)


def quadrants(lat_rows, lon_cols):
    lat_cut, lon_cut = WH // 2, WW // 2
    high_lat, low_lat = slice(lat_cut, lat_rows), slice(lat_cut)
    high_lon, low_lon = slice(lon_cut, lon_cols), slice(lon_cut)
    return (high_lat, high_lon), (high_lat, low_lon), (low_lat, high_lon), (low_lat, low_lon)


def window_matrix(levels, room):
    lat_cut, lon_cut, level_cut = WH // 2, WW // 2, WZ // 2
    count = levels // WZ * WIN
    token = columns((count, 1), 0)
    window = quotient(token, WIN)
    inside = token - window * WIN
    lon = quotient(inside, BLOCK)
    cell = inside - lon * BLOCK
    depth = quotient(cell, WH)
    lat = cell - depth * WH
    level = window * WZ + depth + level_cut
    level = jnp.where(level >= levels, level - levels, level)
    late_lon, late_lat = lon >= lon_cut, lat >= lat_cut
    quad = jnp.where(late_lat, 2, 0) + jnp.where(late_lon, 1, 0)
    row = jnp.where(late_lat, lat - lat_cut, lat)
    col = jnp.where(late_lon, lon - lon_cut, lon)
    source = ((quad * lat_cut + row) * lon_cut + col) * room + level
    return hot(columns((count, WIN // WZ * room), 1) == source)


def pack_body(count, *refs):
    features, cotangent, *plain = refs[: count + 2]
    *outs, sems = refs[count + 2 :]
    lat_rows, lon_cols, _, _ = features.shape
    pairs = []
    for (rows, cols), out in zip(quadrants(lat_rows, lon_cols), outs):
        pairs += [(features.at[rows, cols], out.at[0]), (cotangent.at[rows, cols], out.at[1])]
    pairs += zip(plain, outs[4:])
    copies = [pltpu.make_async_copy(*pair, sems.at[at]) for at, pair in enumerate(pairs)]
    for copy in copies:
        copy.start()
    for copy in copies:
        copy.wait()


def unpack_body(here, from_lon, from_lat, from_both, outputs, grad_features):
    lat_rows, lon_cols, levels, width = outputs.shape
    for (rows, cols), quad in zip(
        quadrants(lat_rows, lon_cols), (here, from_lon, from_lat, from_both)
    ):
        tiles = quad[...].astype(f32).reshape(3, -1, LANES)
        rest = width - LANES
        pair = (
            jnp.concatenate((tiles[0], tiles[2][:, :rest]), 1),
            jnp.concatenate((tiles[1], tiles[2][:, rest:]), 1),
        )
        for value, out in zip(pair, (outputs, grad_features)):
            value = value.reshape(WH // 2, WW // 2, levels, width)
            out[rows, cols] = value.astype(bf16)


def spread_index(index_table):
    parts = []
    rows = [
        jnp.concatenate([index_table[c * WW + a : c * WW + a + 1, :] for c in range(BLOCK)], 0)
        for a in (WW - 1, 0)
    ]
    fill = jnp.zeros((16 - BLOCK, WIN), f32)
    token = columns((WIN, 1), 0)
    cell = quotient(token, WW)
    entry = (token - cell * WW) * BLOCK + cell
    wide = columns((WIN, SPREAD), 1)
    cut_at = (WW - 1) * BLOCK
    picks = (
        hot(jnp.logical_and(entry == wide, wide < cut_at)),
        hot(entry + cut_at == wide),
    )
    for cut in (lambda v: v >> 7, lambda v: v & (LANES - 1)):
        total = jnp.zeros((16, SPREAD), f32)
        for labels, pick in zip(rows, picks):
            value = jnp.concatenate((cut(labels).astype(f32), fill), 0).astype(bf16)
            total += jnp.dot(value, pick, preferred_element_type=f32)
        parts.append(total.astype(jnp.int32))
    return parts


def bias_body(bias_table, index_table, out, chunk_out, lane_out, table):
    level_win, heads, _, labels = bias_table.shape
    chunk, lane = spread_index(index_table)
    chunk_out[...] = chunk
    lane_out[...] = lane
    chunks = -(-labels // LANES)
    for t in range(level_win):
        for h in range(heads):
            table[t * heads + h : t * heads + h + 1, :labels] = bias_table[t, h]
    cell = columns((16, 1), 0)
    other = columns((1, SPREAD), 1)
    other = other - quotient(other, BLOCK) * BLOCK
    level_apart = (cell >= WH) != (other >= WH)
    cell = jnp.where(cell >= WH, cell - WH, cell)
    other = jnp.where(other >= WH, other - WH, other)
    row_apart = (cell >= WH // 2) != (other >= WH // 2)
    top = lax.axis_index("lat") == lax.axis_size("lat") - 1
    barred_rows = jnp.logical_and(row_apart, top)
    rest = BLOCK - SUBLANES
    sub = columns((SUBLANES, LANES), 0)
    early = sub < rest

    def spread_row(row):
        return jnp.broadcast_to(row, (SUBLANES, LANES))

    def take(source, index):
        return jnp.take_along_axis(source, index, axis=1, mode="promise_in_bounds")

    tiles = SPREAD // LANES - 1
    upper, lower = [], []
    for tile in range(tiles):
        at = slice(tile * LANES, (tile + 1) * LANES)
        upper.append((chunk[:SUBLANES, at], lane[:SUBLANES, at]))
        lower.append(
            tuple(
                jnp.concatenate((v[SUBLANES:BLOCK, at], v[SUBLANES:BLOCK, at]), 0)
                for v in (chunk, lane)
            )
        )
    per = BLOCK // 2
    tails = []
    for first in (0, per):
        packed = []
        for v in (chunk, lane):
            total = v[first : first + 1, tiles * LANES :]
            for i in range(1, per):
                row = v[first + i : first + i + 1, tiles * LANES :]
                total = total + pltpu.roll(row, i * TAIL, 1)
            packed.append(spread_row(total))
        tails.append(packed)
    mixed_tail = [jnp.where(early, x, y) for x, y in zip(*tails)]
    rows = level_win * heads
    tail_found = [jnp.zeros((SUBLANES, LANES), f32) for _ in range(3)]
    for c in range(chunks):
        at = slice(c * LANES, (c + 1) * LANES)
        first = table[:SUBLANES, at]
        second = jnp.concatenate((table[SUBLANES:rows, at], table[SUBLANES:rows, at]), 0)
        for k, (source, (which, spot)) in enumerate(
            ((first, tails[0]), (first, tails[1]), (second, mixed_tail))
        ):
            tail_found[k] = jnp.where(which == c, take(source, spot), tail_found[k])
    cell = columns((SUBLANES, LANES), 0)
    entry = columns((SUBLANES, LANES), 1)
    upper_spot = (jnp.where(cell >= per, cell - per, cell) * TAIL + entry) & (LANES - 1)
    lower_cell = jnp.where(early, cell, cell - rest) + SUBLANES - per
    lower_spot = (lower_cell * TAIL + entry) & (LANES - 1)

    for row in range(0, rows, 2):
        pair = (row, row + 1)
        found = [[jnp.zeros((SUBLANES, LANES), f32) for _ in range(3)] for _ in range(tiles)]
        for c in range(chunks):
            sources = [
                spread_row(table[r : r + 1, c * LANES : (c + 1) * LANES]) for r in pair
            ]
            sources.append(jnp.where(early, *sources))
            for tile in range(tiles):
                for k, (which, spot) in enumerate((upper[tile], upper[tile], lower[tile])):
                    found[tile][k] = jnp.where(which == c, take(sources[k], spot), found[tile][k])
        ends = []
        for r in pair:
            if r < SUBLANES:
                ends.append([spread_row(tail_found[k][r : r + 1]) for k in range(2)])
            else:
                at = r - SUBLANES
                ends.append([spread_row(tail_found[2][i : i + 1]) for i in (at, rest + at)])
        last = [take(jnp.where(sub < per, *end), upper_spot) for end in ends]
        last.append(take(jnp.where(early, ends[0][1], ends[1][1]), lower_spot))
        found.append(last)
        for k, r in enumerate(pair):
            value = jnp.concatenate(
                [jnp.concatenate((f[k], f[2][k * rest : (k + 1) * rest]), 0) for f in found], 1
            )
            barred = barred_rows
            if r // heads == level_win - 1:
                barred = jnp.logical_or(barred, level_apart)
            value = jnp.where(barred[:BLOCK], -LARGE, value)
            for a in range(WW):
                shift = (WW - 1 - a) * BLOCK
                out[r, a * BLOCK : (a + 1) * BLOCK, :] = value[:, shift : shift + WIN]


def inverse_body(chunk, lane, chunk_out, lane_out):
    pieces = SPREAD // LANES
    labels = chunk_out.shape[0]
    valid = SPANS * BLOCK
    total = jnp.zeros((2 * labels, LANES), f32)
    wide = lax.broadcasted_iota(jnp.int32, (labels, SPREAD), 1)
    tall = lax.broadcasted_iota(jnp.int32, (labels, SPREAD), 0)
    lanes = lax.broadcasted_iota(jnp.int32, (LANES, SPREAD), 0)
    for cell in range(BLOCK):
        own = jnp.logical_and(chunk[cell : cell + 1, :] == tall, wide < valid)
        piece = jnp.where(own, (cell * pieces + wide // LANES).astype(f32), 0.0)
        spot = jnp.where(own, (wide % LANES).astype(f32), 0.0)
        both = jnp.concatenate((piece, spot), 0).astype(bf16)
        hit = jnp.where(lane[cell : cell + 1, :] == lanes, 1.0, 0.0).astype(bf16)
        total += lax.dot_general(both, hit, (((1,), (1,)), ((), ())), preferred_element_type=f32)
    chunk_out[...] = total[:labels].astype(jnp.int32)
    lane_out[...] = total[labels:].astype(jnp.int32)


def place_body(blocks, piece, spot, out):
    pieces = SPREAD // LANES
    head = columns((SUBLANES, 1), 0)
    at_piece, at_spot, at_tail = [], [], []
    for c in range(out.shape[1] // LANES):
        at_piece.append(jnp.broadcast_to(piece[c : c + 1, :], (SUBLANES, LANES)))
        at_spot.append(jnp.broadcast_to(spot[c : c + 1, :], (SUBLANES, LANES)))
        at_tail.append((at_spot[c] + TAIL * head) & (LANES - 1))
    found = [jnp.zeros((SUBLANES, LANES), f32) for _ in at_piece]
    values = blocks[...].astype(f32).reshape(TABLE_ROWS, LANES)
    fill = jnp.zeros((SUBLANES - HEADS, LANES), f32)
    for cell in range(BLOCK):
        for tile in range(pieces):
            if tile < pieces - 1:
                starts = [(tile * HEADS + h) * BLOCK + cell for h in range(HEADS)]
                source = jnp.concatenate([values[r : r + 1] for r in starts] + [fill], 0)
                spots = at_spot
            else:
                row = tile * HEADS * BLOCK + cell
                source = jnp.broadcast_to(values[row : row + 1], (SUBLANES, LANES))
                spots = at_tail
            for c in range(len(found)):
                taken = jnp.take_along_axis(source, spots[c], axis=1, mode="promise_in_bounds")
                found[c] = jnp.where(at_piece[c] == cell * pieces + tile, taken, found[c])
    for c in range(len(found)):
        out[:, c * LANES : (c + 1) * LANES] = found[c].astype(bf16)


def window_body(
    here, from_lon, from_lat, from_both, norm_gain, norm_shift, w_qkv, w_out, bias,
    out_here, out_lon, out_lat, out_both, keep, send, gathered, proj_grad, sums, tables,
):
    width = w_out.shape[0]
    level_win = bias.shape[0] // HEADS
    head_size = width // HEADS
    scaling = head_size ** (-0.5)
    _, lat_half, lon_half, levels, _ = here.shape
    quad_rows = lat_half * lon_half * PAD_LEVEL
    fill = jnp.zeros((lat_half, lon_half, PAD_LEVEL - levels, width), f32)
    picks = window_matrix(levels, PAD_LEVEL)
    features, cotangent = (
        jnp.dot(
            picks,
            jnp.concatenate(
                [
                    jnp.concatenate((quad[at].astype(f32), fill), 2).reshape(quad_rows, width)
                    for quad in (here, from_lon, from_lat, from_both)
                ],
                0,
            ).astype(bf16),
            preferred_element_type=f32,
        )
        for at in range(2)
    )
    grad_shifted = cotangent.astype(bf16)
    gain = norm_gain[...]
    center = features - jnp.mean(features, -1, keepdims=True)
    inv_std = lax.rsqrt(jnp.mean(center * center, -1, keepdims=True) + epsilon)
    x_hat = center * inv_std
    normed = (x_hat * gain + norm_shift[...]).astype(bf16)
    query, key, value = (
        jnp.dot(normed, w_qkv[:, k * width : (k + 1) * width], preferred_element_type=f32).astype(bf16)
        for k in range(3)
    )
    grad_heads = lax.dot_general(
        grad_shifted, w_out[...], (((1,), (1,)), ((), ())), preferred_element_type=f32
    ).astype(bf16)
    head_of = lax.broadcasted_iota(jnp.int32, (1, width), 1) // head_size
    mixed_parts = []
    for t in range(level_win):
        rows = slice(t * WIN, (t + 1) * WIN)
        q, k, v, g = query[rows], key[rows], value[rows], grad_heads[rows]
        q_heads = [jnp.where(head_of == h, q, jnp.zeros_like(q)) for h in range(HEADS)]
        g_heads = [jnp.where(head_of == h, g, jnp.zeros_like(g)) for h in range(HEADS)]
        q_heads = jnp.concatenate(q_heads, 0)
        g_heads = jnp.concatenate(g_heads, 0)
        all_logits = lax.dot_general(
            q_heads, k, (((1,), (1,)), ((), ())), preferred_element_type=f32
        )
        all_grads = lax.dot_general(
            g_heads, v, (((1,), (1,)), ((), ())), preferred_element_type=f32
        )
        mixed = jnp.zeros((WIN, width), f32)
        grad_query = jnp.zeros((WIN, width), f32)
        all_weights, all_logit_grads = [], []
        for h in range(HEADS):
            span = slice(h * WIN, (h + 1) * WIN)
            logits = all_logits[span] * scaling + bias[t * HEADS + h]
            raised = jnp.exp(logits - jnp.max(logits, -1, keepdims=True))
            weights = raised * (1.0 / jnp.sum(raised, -1, keepdims=True))
            weights_bf = weights.astype(bf16)
            mixed = jnp.where(
                head_of == h, jnp.dot(weights_bf, v, preferred_element_type=f32), mixed
            )
            grad_weights = all_grads[span]
            grad_logits = weights * (
                grad_weights - jnp.sum(weights * grad_weights, -1, keepdims=True)
            )
            logit_bf = grad_logits.astype(bf16)
            grad_query = jnp.where(
                head_of == h, jnp.dot(logit_bf, k, preferred_element_type=f32), grad_query
            )
            all_weights.append(weights_bf)
            all_logit_grads.append(logit_bf)
            total = jnp.zeros((BLOCK, SPREAD), f32)
            for a in range(WW):
                shift = (WW - 1 - a) * BLOCK
                piece = grad_logits[a * BLOCK : (a + 1) * BLOCK]
                piece = jnp.concatenate((piece, jnp.zeros((BLOCK, SPREAD - WIN), f32)), 1)
                total += pltpu.roll(piece, shift, 1) if shift else piece
            for tile in range(2):
                row = (tile * HEADS + h) * BLOCK
                tables[t, row : row + BLOCK, :] = total[:, tile * LANES : (tile + 1) * LANES]
            last = total[:, 2 * LANES :]
            tails = tails + pltpu.roll(last, h * TAIL, 1) if h else last
        row = 2 * HEADS * BLOCK
        tables[t, row : row + BLOCK, :] = tails
        tables[t, row + BLOCK :, :] = jnp.zeros((TABLE_ROWS - row - BLOCK, LANES), f32)
        grad_value, grad_key = (
            lax.dot_general(
                jnp.concatenate(left, 0), right, (((0,), (0,)), ((), ())), preferred_element_type=f32
            )
            for left, right in ((all_weights, g_heads), (all_logit_grads, q_heads))
        )
        mixed_parts.append(mixed.astype(bf16))
        proj_grad[rows, :width] = (grad_query * scaling).astype(bf16)
        proj_grad[rows, width : 2 * width] = (grad_key * scaling).astype(bf16)
        proj_grad[rows, 2 * width :] = grad_value.astype(bf16)
    mixed = jnp.concatenate(mixed_parts, 0)
    attn = jnp.dot(mixed, w_out[...], preferred_element_type=f32).astype(bf16)
    outputs = (features + attn.astype(f32)).astype(bf16)
    grad_proj = proj_grad[...]
    grad_input = lax.dot_general(
        grad_proj, w_qkv[...], (((1,), (1,)), ((), ())), preferred_element_type=f32
    )
    upstream = grad_input.astype(bf16).astype(f32)
    gain_part = jnp.sum(upstream * x_hat, 0, keepdims=True)
    shift_part = jnp.sum(upstream, 0, keepdims=True)
    g_hat = upstream * gain
    centred = (
        g_hat
        - jnp.mean(g_hat, -1, keepdims=True)
        - x_hat * jnp.mean(g_hat * x_hat, -1, keepdims=True)
    )
    grad_features = (cotangent + inv_std * centred).astype(bf16)
    picks = window_matrix(levels, levels)
    back = [
        lax.dot_general(picks, result, (((0,), (0,)), ((), ())), preferred_element_type=f32)
        for result in (outputs, grad_features)
    ]
    rest = width - LANES
    tiles = [b[:, :LANES] for b in back]
    tiles.append(jnp.concatenate([b[:, LANES:] for b in back], 1))
    groups = lat_half * lon_half * levels // SUBLANES
    for at, tile in enumerate(tiles):
        tile = tile.astype(bf16).reshape(4, groups, SUBLANES, LANES)
        for q, out in enumerate((out_here, out_lon, out_lat, out_both)):
            out[at * groups : (at + 1) * groups] = tile[q]
    sums[:, : 3 * width] = lax.dot_general(
        normed, grad_proj, (((0,), (0,)), ((), ())), preferred_element_type=f32
    )
    sums[:, 3 * width :] = lax.dot_general(
        mixed, grad_shifted, (((0,), (0,)), ((), ())), preferred_element_type=f32
    )
    chunks, blocks, _, _ = gathered.shape
    lat_count = chunks // 2
    size = width // chunks
    fill = jnp.zeros((1, 2 * LANES - width), f32)
    ends = [gain_part[:, :LANES], jnp.concatenate((gain_part[:, LANES:], fill), 1)]
    ends += [shift_part[:, :LANES], jnp.concatenate((shift_part[:, LANES:], fill), 1)]
    ends = jnp.concatenate(ends + [jnp.zeros((SUBLANES - 4, LANES), f32)], 0).astype(bf16)
    for j in range(chunks):
        piece = jnp.concatenate(
            [
                sums[j * size : (j + 1) * size, b * LANES : (b + 1) * LANES]
                for b in range(4 * width // LANES)
            ],
            0,
        )
        gathered[j, : blocks - 1] = piece.reshape(blocks - 1, SUBLANES, LANES).astype(bf16)
        gathered[j, blocks - 1] = ends
    core = lax.axis_index("lon") % 2
    lat = lax.axis_index("lat")
    for half, out in enumerate((keep, send)):
        side = core ^ half
        for at in range(lat_count):
            out[at * blocks : (at + 1) * blocks] = gathered[
                side * lat_count + (lat ^ at)
            ]
        table = tables[side].reshape(TABLE_ROWS // SUBLANES, SUBLANES, LANES)
        out[lat_count * blocks :] = table.astype(bf16)


def tree(values):
    while len(values) > 1:
        values = [a + b for a, b in zip(values[::2], values[1::2])]
    return values[0]


def halves_body(keep, came, *outs):
    at = 0
    for out in outs:
        part = slice(at, at + out.shape[0])
        out[...] = (keep[part].astype(f32) + came[part].astype(f32)).astype(bf16)
        at += out.shape[0]


def lats_body(*refs):
    *pieces, tail, out = refs
    blocks = pieces[0].shape[0]
    out[:blocks] = tree([p[...].astype(f32) for p in pieces]).astype(bf16)
    out[blocks:] = tail[...]


def lons_body(count, *refs):
    pieces, (weights, tail) = refs[:count], refs[count:]
    blocks = weights.shape[0]
    total = tree([p[...].astype(f32) for p in pieces]).astype(bf16)
    weights[...] = total[:blocks]
    tail[...] = total[blocks:]


def finish_body(lat_count, factor, *refs):
    near, far = refs[:lat_count], refs[lat_count : 2 * lat_count]
    table_near, table_far, grad_gain, grad_shift, grad_wqkv, grad_wout, grad_table, chunks, halves = refs[
        2 * lat_count :
    ]
    core = lax.axis_index("lon") % 2
    lat = lax.axis_index("lat")
    count, blocks, _, _ = chunks.shape
    for half, group in enumerate((near, far)):
        for at, ref in enumerate(group):
            chunks[(core ^ half) * lat_count + (lat ^ at)] = ref[...].astype(f32) * factor
    halves[core] = table_near[...].astype(f32) * factor
    halves[core ^ 1] = table_far[...].astype(f32) * factor
    width = grad_wout.shape[0]
    size = width // count
    for j in range(count):
        rows = slice(j * size, (j + 1) * size)
        tall = chunks[j, : blocks - 1].reshape((blocks - 1) * SUBLANES, LANES)
        whole = jnp.concatenate(
            [tall[b * size : (b + 1) * size] for b in range(tall.shape[0] // size)], 1
        )
        grad_wqkv[rows, :] = whole[:, : 3 * width]
        grad_wout[rows, :] = whole[:, 3 * width :]
    rest = width - LANES
    for at, out in enumerate((grad_gain, grad_shift)):
        out[:, :LANES] = chunks[0, blocks - 1, 2 * at : 2 * at + 1]
        out[:, LANES:] = chunks[0, blocks - 1, 2 * at + 1 : 2 * at + 2, :rest]
    level_win, heads, _, labels = grad_table.shape
    for t in range(level_win):
        for h in range(heads):
            grad_table[t, h] = halves[t, h : h + 1, :labels]


def swap(value, axis, distance):
    count = lax.axis_size(axis)
    return lax.ppermute(value, axis, [(source, source ^ distance) for source in range(count)])


def shifted(value, lat_step, lon_step):
    lat_count, lon_count = lax.axis_size("lat"), lax.axis_size("lon")
    pairs = [
        (r * lon_count + c, (r + lat_step) % lat_count * lon_count + (c + lon_step) % lon_count)
        for r in range(lat_count)
        for c in range(lon_count)
    ]
    return lax.ppermute(value, ("lat", "lon"), pairs)


def on_device(features, norm_gain, norm_shift, w_qkv, w_out, bias_table, index_table, cotangent):
    levels, lat_rows, lon_cols, width = features.shape
    level_win, _, heads, labels = bias_table.shape
    lat_count, lon_count = lax.axis_size("lat"), lax.axis_size("lon")
    quad = struct((2, WH // 2, WW // 2, levels, width), bf16)
    steps = ((0, 1), (1, 0), (1, 1))

    plain = (
        norm_gain[None], norm_shift[None], w_qkv, w_out, bias_table.transpose(0, 2, 1, 3), index_table
    )
    far_side = pl.BlockSpec(memory_space=pltpu.HBM)
    *packed, gain, shift, w_qkv, w_out, table, labels_of = call(
        functools.partial(pack_body, len(plain)),
        (quad,) * 4 + tuple(struct(p.shape, p.dtype) for p in plain),
        [pltpu.SemaphoreType.DMA((8 + len(plain),))],
        in_specs=[far_side] * (2 + len(plain)),
    )(
        *(
            pltpu.with_memory_space_constraint(v, pltpu.HBM)
            for v in (features.transpose(1, 2, 0, 3), cotangent.transpose(1, 2, 0, 3), *plain)
        )
    )
    here, *edges = packed
    came = [shifted(e, -lat, -lon) for e, (lat, lon) in zip(edges, steps)]

    spread = struct((16, SPREAD), jnp.int32)
    whole_lanes = -(-labels // LANES) * LANES
    bias, chunk, lane = call(
        bias_body,
        (struct((level_win * heads, WIN, WIN), f32), spread, spread),
        [pltpu.VMEM((level_win * heads, whole_lanes), f32)],
        moved=16 * 10**6,
    )(table, labels_of)

    blocks = 4 * width * width // (2 * lat_count) // (SUBLANES * LANES) + 1
    table_blocks = TABLE_ROWS // SUBLANES
    quad_blocks = 2 * WH // 2 * WW // 2 * levels * width // (SUBLANES * LANES)

    def stack(count):
        return struct((count, SUBLANES, LANES), bf16)

    half = stack(lat_count * blocks + table_blocks)
    out_here, *backs, keep, send = call(
        window_body,
        (stack(quad_blocks),) * 4 + (half, half),
        [
            pltpu.VMEM((2 * lat_count, blocks, SUBLANES, LANES), bf16),
            pltpu.VMEM((level_win * WIN, 3 * width), bf16),
            pltpu.VMEM((width, 4 * width), f32),
            pltpu.VMEM((level_win, TABLE_ROWS, LANES), f32),
        ],
        moved=25 * 10**6,
    )(here, *came, gain, shift, w_qkv, w_out, bias)

    send, chunk, lane = lax.optimization_barrier((send, chunk, lane))
    came = swap(send, "lon", 1)
    places = struct((32, LANES), jnp.int32)
    piece, spot = call(inverse_body, (places, places), moved=2 * 10**6)(chunk, lane)
    came, piece, spot = lax.optimization_barrier((came, piece, spot))
    *pieces, tail = call(halves_body, (stack(blocks),) * lat_count + (stack(table_blocks),))(keep, came)
    pieces = [swap(p, "lat", at) if at else p for at, p in enumerate(pieces)]
    returned = [shifted(b, lat, lon) for b, (lat, lon) in zip(backs, steps)]
    tail, returned[0] = lax.optimization_barrier((tail, returned[0]))
    part = call(lats_body, stack(blocks + table_blocks))(*pieces, tail)
    parts = [part] + [swap(part, "lon", 2 * at) for at in range(1, lon_count // 2)]
    weights, tail = call(functools.partial(lons_body, len(parts)), (stack(blocks), stack(table_blocks)))(
        *parts
    )
    near = [weights] + [swap(weights, "lat", at) for at in range(1, lat_count)]
    table_near = call(place_body, struct((SUBLANES, whole_lanes), bf16), moved=5 * 10**6)(
        tail, piece, spot
    )
    table_far = swap(table_near, "lon", 1)
    far = [swap(n, "lon", 1) for n in near]

    cells = struct((lat_rows, lon_cols, levels, width), bf16)
    outputs, grad_features = call(unpack_body, (cells, cells), moved=2 * 10**6)(
        out_here, *returned
    )
    factor = (levels * lat_rows * lat_count * lon_cols * lon_count) ** (-0.5)
    row = struct((1, width), f32)
    grad_gain, grad_shift, grad_wqkv, grad_wout, grad_table = call(
        functools.partial(finish_body, lat_count, factor),
        (
            row,
            row,
            struct(w_qkv.shape, f32),
            struct(w_out.shape, f32),
            struct((level_win, heads, 1, labels), f32),
        ),
        [
            pltpu.VMEM((2 * lat_count, blocks, SUBLANES, LANES), f32),
            pltpu.VMEM((2,) + table_near.shape, f32),
        ],
    )(*near, *far, table_near, table_far)
    return (
        outputs.transpose(2, 0, 1, 3),
        grad_features.transpose(2, 0, 1, 3),
        grad_gain[0],
        grad_shift[0],
        grad_wqkv,
        grad_wout,
        grad_table.transpose(0, 2, 1, 3),
    )


def solution(mesh):
    placed = (
        P(None, "lat", "lon", None),
        P(),
        P(),
        P(),
        P(),
        P(None, "lat", None, None),
        P(),
        P(None, "lat", "lon", None),
    )
    return jax.shard_map(
        on_device,
        mesh=mesh,
        in_specs=placed,
        out_specs=(
            P(None, "lat", "lon", None),
            P(None, "lat", "lon", None),
            P(),
            P(),
            P(),
            P(),
            P(None, "lat", None, None),
        ),
        check_vma=False,
    )
```
